512 devices in a mesh: lon: 64 (over z, y_hi, core), lat: 8 (over x, y_lo).
Axes of the slice: x: 4, y: 4 (y_hi: 2, y_lo: 2; y = y_hi * 2 + y_lo), z: 16, core: 2. Of those that a mesh axis runs over, the one named last changes fastest.
Arguments:
- tokens: bfloat16 [1536, 288, 512], P('lon', 'lat'), may hold values from -24 to 24
- norm_gain: float32 [512], replicated, may hold values from 0.1 to 1.9
- w_qkv: bfloat16 [512, 1536], replicated, may hold values from -1.767767 to 1.767767
- w_out: bfloat16 [512, 512], replicated, may hold values from -0.25 to 0.25
- pole_mask: int32 [288], replicated, may hold values from 0 to 1, as said below
Outputs:
- mixed: bfloat16 [1536, 288, 512], P('lon', 'lat')
The draws below stay inside these ranges and needn't reach their ends.
Inputs may be any that keep to these rules, and one draw needn't show every extreme that they name: `pole_mask`: the first t and the last s rows are 0 and all others 1, with t and s between 1 and 5.
All inputs are finite; a program needn't handle non-finite values.
Results may differ from the reference program's by a relative error of at most 0.012.
The reference program's roundings to bfloat16 on the way (of `normed`, `projected`, `probabilities` and `context`) count: a program that leaves them out, or rounds other values in their place, can miss the bound.
Values may be sent and summed in bfloat16 or wider, within the bound.
No kernel may reach another device: no remote copies, remote signals or barrier semaphores. Data moves between devices by JAX's collectives and lax.ppermute only.
A program may use at most 64 MiB of HBM per device.

```python
import math
import jax
import jax.numpy as jnp
from jax import lax

WIDTH = 512
HEADS = 8
WINDOW = 12
SHIFT = 6
NLON = 1536
NLAT = 288


def draw_tokens(key, part):
    key = jax.random.fold_in(key, 11)
    key_base, key_cols, key_rows = jax.random.split(key, 3)
    col_scale = jnp.exp(jax.random.uniform(key_cols, (WIDTH,), jnp.float32, math.log(0.3), math.log(3.0)))
    row_scale = jnp.exp(jax.random.uniform(key_rows, (NLON, NLAT, 1), jnp.float32, math.log(0.5), math.log(2.0)))
    base = jnp.clip(jax.random.normal(key_base, (NLON, NLAT, WIDTH), jnp.float32), -4.0, 4.0)
    return (base * col_scale * row_scale).astype(jnp.bfloat16)


def draw_w_qkv(key, part):
    key = jax.random.fold_in(key, 23)
    key_base = jax.random.fold_in(key, 0)
    base = jnp.clip(jax.random.normal(key_base, (WIDTH, 3 * WIDTH), jnp.float32), -4.0, 4.0) * WIDTH ** (-0.5)
    return base.astype(jnp.bfloat16)


def draw_pole_mask(key, part):
    key = jax.random.fold_in(key, 37)
    key_top, key_bottom = jax.random.split(key)
    top_rows = jax.random.randint(key_top, (), 1, 6)
    bottom_rows = jax.random.randint(key_bottom, (), 1, 6)
    latitude = jnp.arange(NLAT, dtype=jnp.int32)
    return ((latitude >= top_rows) & (latitude < NLAT - bottom_rows)).astype(jnp.int32)


def gaussian(own_key, dims, deviation, limit, held_as=jnp.bfloat16):
    values = deviation * jax.random.normal(own_key, dims, jnp.float32)
    return jnp.clip(values, min=-limit, max=limit).astype(held_as)


def setup_inputs(seed: int = 0) -> dict:
    key_list = jax.random.split(jax.random.key(seed), 6)
    tokens = draw_tokens(jax.random.fold_in(key_list[5], 71), 0)
    norm_gain = jnp.clip(1.0 + 0.18 * jax.random.normal(key_list[1], (WIDTH,), jnp.float32), 0.1, 1.9)
    w_qkv = draw_w_qkv(jax.random.fold_in(key_list[5], 71), 0)
    w_out = gaussian(key_list[3], (WIDTH, WIDTH), WIDTH ** -0.5, 0.25)
    pole_mask = draw_pole_mask(jax.random.fold_in(key_list[5], 71), 0)
    return {"tokens": tokens, "norm_gain": norm_gain, "w_qkv": w_qkv, "w_out": w_out, "pole_mask": pole_mask}


EPS = 1e-05

def layer_norm(tokens, norm_gain):
    values32 = tokens.astype(jnp.float32)
    average = lax.optimization_barrier(jnp.mean(values32, axis=-1, keepdims=True))
    centred = values32 - average
    variance = lax.optimization_barrier(jnp.mean(centred * centred, axis=-1, keepdims=True))
    return (centred * lax.rsqrt(variance + EPS) * norm_gain.astype(jnp.float32)).astype(jnp.bfloat16)

def window_attend(queries, key_part, value_part, key_usable):
    head_size = queries.shape[-1]
    scores = jnp.einsum('nqhd,nkhd->nhqk', queries.astype(jnp.float32), key_part.astype(jnp.float32), precision=lax.Precision.HIGHEST)
    scores = scores * head_size ** (-0.5)
    scores = jnp.where(key_usable[None, None, None, :], scores, -1e+30)
    row_max = lax.optimization_barrier(jnp.max(scores, axis=-1, keepdims=True))
    exp_scores = jnp.exp(scores - row_max)
    probabilities = (exp_scores / lax.optimization_barrier(jnp.sum(exp_scores, axis=-1, keepdims=True))).astype(jnp.bfloat16)
    context = jnp.einsum('nhqk,nkhd->nqhd', probabilities.astype(jnp.float32), value_part.astype(jnp.float32), precision=lax.Precision.HIGHEST)
    return context.astype(jnp.bfloat16)

def reference(tokens, norm_gain, w_qkv, w_out, pole_mask):
    width = tokens.shape[-1]
    head_size = width // HEADS
    normed = layer_norm(tokens, norm_gain)
    projected = jnp.dot(normed.reshape(-1, width), w_qkv, preferred_element_type=jnp.float32).astype(jnp.bfloat16)
    projected = projected.reshape(NLON, NLAT, 3 * width)
    rolled = jnp.roll(projected, SHIFT, axis=0)
    padded = jnp.pad(rolled, ((0, 0), (SHIFT, SHIFT), (0, 0)))
    usable_rows = jnp.pad(pole_mask == 1, (SHIFT, SHIFT))
    lat_windows = (NLAT + 2 * SHIFT) // WINDOW
    lon_windows = NLON // WINDOW

    def attend_rows(window_index):
        start = (window_index * WINDOW).astype(jnp.int32)
        window_rows = lax.dynamic_slice_in_dim(padded, start, WINDOW, 1)
        window_rows = window_rows.reshape(lon_windows, WINDOW * WINDOW, 3 * width)
        queries = window_rows[:, :, :width].reshape(lon_windows, WINDOW * WINDOW, HEADS, head_size)
        key_part = window_rows[:, :, width:2 * width].reshape(lon_windows, WINDOW * WINDOW, HEADS, head_size)
        value_part = window_rows[:, :, 2 * width:].reshape(lon_windows, WINDOW * WINDOW, HEADS, head_size)
        key_usable = jnp.tile(lax.dynamic_slice_in_dim(usable_rows, start, WINDOW, 0), WINDOW)
        context = window_attend(queries, key_part, value_part, key_usable)
        return context.reshape(NLON, WINDOW, width)
    stacked = lax.map(attend_rows, jnp.arange(lat_windows, dtype=jnp.int32))
    context = jnp.transpose(stacked, (1, 0, 2, 3)).reshape(NLON, lat_windows * WINDOW, width)
    context = jnp.roll(context[:, SHIFT:SHIFT + NLAT], -SHIFT, axis=0)
    update = jnp.dot(context.reshape(-1, width), w_out, preferred_element_type=jnp.float32)
    mixed = tokens.reshape(-1, width).astype(jnp.float32) + update
    return mixed.reshape(NLON, NLAT, width).astype(jnp.bfloat16)
```

```python
import functools

import jax
import jax.numpy as jnp
from jax import lax
from jax.experimental import pallas as pl
from jax.experimental.pallas import tpu as pltpu
from jax.sharding import PartitionSpec as P

WIDTH = 512
HEADS = 8
WINDOW = 12
SHIFT = 6
KEYS = WINDOW * WINDOW
EPS = 1e-05
LON = 24
LAT = 36
EDGE = LAT * SHIFT
BF = jnp.bfloat16
F32 = jnp.float32


def normalise(window_tokens, gain, normed, rows):
    block = 144
    for start in range(0, rows, block):
        values = window_tokens[start : start + block, :]
        average = jnp.sum(values, axis=-1, keepdims=True) * (1.0 / WIDTH)
        centred = values - average
        variance = jnp.sum(centred * centred, axis=-1, keepdims=True) * (1.0 / WIDTH)
        normed[start : start + block, :] = (centred * lax.rsqrt(variance + EPS) * gain).astype(BF)


def attend(window_tokens, gain_ref, w_qkv, w_out, counts, bias, normed, q_rows, pairs, queries, context, mixed):
    total = KEYS * len(counts)
    normalise(window_tokens, gain_ref[...], normed, total)
    offsets = []
    here = 0
    for index, count in enumerate(counts):
        offsets.append(here)
        q_rows[here : here + count, :] = normed[KEYS * index : KEYS * index + count, :]
        here += count
    asked = here
    for col in range(0, 2 * WIDTH, 256):
        part = jnp.dot(normed[...], w_qkv[:, WIDTH + col : WIDTH + col + 256], preferred_element_type=F32)
        pairs[:, col : col + 256] = part.astype(BF)
    for col in range(0, WIDTH, 256):
        part = jnp.dot(q_rows[...], w_qkv[:, col : col + 256], preferred_element_type=F32)
        queries[:, col : col + 256] = (part.astype(BF).astype(F32) * (WIDTH // HEADS) ** (-0.5)).astype(BF)
    lane = lax.broadcasted_iota(jnp.int32, (1, 128), 1)
    low32 = lane < 64
    keep_low = low32.astype(F32).astype(BF)
    keep_high = (lane >= 64).astype(F32).astype(BF)
    ones = jnp.ones((KEYS, 128), BF)
    for index, count in enumerate(counts):
        base, q_base = KEYS * index, offsets[index]
        for pair in range(HEADS // 2):
            cols = slice(128 * pair, 128 * pair + 128)
            both = queries[q_base : q_base + count, cols]
            stacked = jnp.concatenate([both * keep_low, both * keep_high], axis=0)
            key_part = pairs[base : base + KEYS, cols]
            value_part = pairs[base : base + KEYS, WIDTH + 128 * pair : WIDTH + 128 * pair + 128]
            scores = lax.dot_general(stacked, key_part, (((1,), (1,)), ((), ())), preferred_element_type=F32)
            if bias is not None:
                scores = scores + bias[index]
            row_max = jnp.max(scores, axis=-1, keepdims=True)
            exp_scores = jnp.exp(scores - row_max).astype(BF)
            widened = jnp.concatenate([value_part, ones], axis=1)
            summed = jnp.dot(exp_scores, widened, preferred_element_type=F32)
            first, second = summed[:count], summed[count:]
            top = jnp.where(low32, first[:, :128], second[:, :128])
            under = jnp.where(low32, first[:, 128:], second[:, 128:])
            context[q_base : q_base + count, cols] = (top / under).astype(BF)
    for col in range(0, WIDTH, 256):
        part = jnp.dot(context[...], w_out[:, col : col + 256], preferred_element_type=F32)
        for index, count in enumerate(counts):
            q_base = offsets[index]
            mixed[q_base : q_base + count, col : col + 256] = (
                part[q_base : q_base + count] + window_tokens[KEYS * index : KEYS * index + count, col : col + 256]
            )
    return offsets


def pack_lon(x, east, west, east32, west32):
    for lat in range(LAT):
        row = x[lat].astype(F32)
        west32[SHIFT * lat : SHIFT * lat + SHIFT, :] = row[0:SHIFT]
        east32[SHIFT * lat : SHIFT * lat + SHIFT, :] = row[LON - SHIFT : LON]
    west[...] = west32[...].astype(BF)
    east[...] = east32[...].astype(BF)


def pack_lat(x, from_west, from_east, north, south, work):
    own = SHIFT * LON
    for target, lat, halo in ((south, 0, 0), (north, LAT - SHIFT, EDGE - 36)):
        target[0:own, :] = x[lat : lat + SHIFT].reshape(own, WIDTH)
        work[0:36, :] = from_west[...].astype(F32)[halo : halo + 36]
        work[36:72, :] = from_east[...].astype(F32)[halo : halo + 36]
        target[own : own + 72, :] = work[...].astype(BF)


def middle(x, gain, w_qkv, w_out, out, x32, stack, normed, q_rows, pairs, queries, context, mixed):
    x32[...] = x[SHIFT : LAT - SHIFT].astype(F32)
    for lat in range(24):
        stack[12 * lat : 12 * lat + 12, :] = x32[lat, 6:18, :]
    attend(stack, gain, w_qkv, w_out, (144, 144), None, normed, q_rows, pairs, queries, context, mixed)
    for lat in range(24):
        x32[lat, 6:18, :] = mixed[12 * lat : 12 * lat + 12, :]
    out[...] = x32[...].astype(BF)


def sides(x, from_west, from_east, done, gain, w_qkv, w_out, out, x32, w32, e32, stack, normed, q_rows, pairs, queries, context, mixed):
    x32[...] = x[SHIFT : LAT - SHIFT].astype(F32)
    w32[...] = from_west[...].astype(F32)
    e32[...] = from_east[...].astype(F32)
    for index in range(4):
        band, east = index // 2, index % 2
        lon = 18 if east else 0
        base = KEYS * index
        for step in range(12):
            stack[base + 6 * step : base + 6 * step + 6, :] = x32[12 * band + step, lon : lon + 6, :]
        halo = e32 if east else w32
        stack[base + 72 : base + 144, :] = halo[36 + 72 * band : 108 + 72 * band, :]
    offsets = attend(stack, gain, w_qkv, w_out, (80,) * 4, None, normed, q_rows, pairs, queries, context, mixed)
    x32[...] = done[...].astype(F32)
    for index in range(4):
        band, east = index // 2, index % 2
        lon = 18 if east else 0
        for step in range(12):
            x32[12 * band + step, lon : lon + 6, :] = mixed[offsets[index] + 6 * step : offsets[index] + 6 * step + 6, :]
    out[...] = x32[...].astype(BF)


def poles(
    mask, x, from_west, from_east, from_south, from_north, done, gain, w_qkv, w_out, out,
    x32, w32, e32, s32, n32, stack, normed, q_rows, pairs, queries, context, mixed,
):
    x32[0:SHIFT] = x[0:SHIFT].astype(F32)
    x32[SHIFT : 2 * SHIFT] = x[LAT - SHIFT : LAT].astype(F32)
    w32[...] = from_west[...].astype(F32)
    e32[...] = from_east[...].astype(F32)
    s32[...] = from_south[...].astype(F32)
    n32[...] = from_north[...].astype(F32)
    band = lax.axis_index("lat")
    first = band * LAT
    key = lax.broadcasted_iota(jnp.int32, (1, KEYS), 1)
    in_halo = key >= 72
    inner = jnp.where(in_halo, key - 72, key)
    row_wide = inner // 12
    row_corner = jnp.where(inner >= 36, inner - 36, inner) // 6
    biases = []
    counts = []
    for north in range(2):
        halo = n32 if north else s32
        lat_at = first + LAT - SHIFT if north else first
        halo_at = first + LAT if north else first - SHIFT
        bias_wide = jnp.zeros((1, KEYS), F32)
        bias_corner = jnp.zeros((1, KEYS), F32)
        for step in range(SHIFT):
            own_ok = mask[lat_at + step] == 1
            there = halo_at + step
            exists = jnp.logical_and(there >= 0, there < 288)
            halo_ok = jnp.logical_and(exists, mask[jnp.clip(there, 0, 287)] == 1)
            own_bias = jnp.where(own_ok, 0.0, -1e30)
            halo_bias = jnp.where(halo_ok, 0.0, -1e30)
            step_bias = jnp.where(in_halo, halo_bias, own_bias)
            bias_wide = jnp.where(row_wide == step, step_bias, bias_wide)
            bias_corner = jnp.where(row_corner == step, step_bias, bias_corner)
        base = 3 * KEYS * north
        for step in range(SHIFT):
            row = x32[SHIFT * north + step]
            edge = halo[LON * step : LON * step + LON]
            stack[base + 12 * step : base + 12 * step + 12, :] = row[6:18]
            stack[base + 72 + 12 * step : base + 84 + 12 * step, :] = edge[6:18]
            stack[base + 144 + 6 * step : base + 150 + 6 * step, :] = row[0:6]
            stack[base + 216 + 6 * step : base + 222 + 6 * step, :] = edge[0:6]
            stack[base + 288 + 6 * step : base + 294 + 6 * step, :] = row[18:24]
            stack[base + 360 + 6 * step : base + 366 + 6 * step, :] = edge[18:24]
        at = EDGE - 36 if north else 0
        stack[base + 180 : base + 216, :] = w32[at : at + 36, :]
        stack[base + 252 : base + 288, :] = halo[144:180, :]
        stack[base + 324 : base + 360, :] = e32[at : at + 36, :]
        stack[base + 396 : base + 432, :] = halo[180:216, :]
        biases += [bias_wide, bias_corner, bias_corner]
        counts += [80, 48, 48]
    offsets = attend(stack, gain, w_qkv, w_out, tuple(counts), biases, normed, q_rows, pairs, queries, context, mixed)
    for north in range(2):
        wide, west, east = offsets[3 * north : 3 * north + 3]
        for step in range(SHIFT):
            at = SHIFT * north + step
            x32[at, 6:18, :] = mixed[wide + 12 * step : wide + 12 * step + 12, :]
            x32[at, 0:6, :] = mixed[west + 6 * step : west + 6 * step + 6, :]
            x32[at, 18:24, :] = mixed[east + 6 * step : east + 6 * step + 6, :]
    out[0:SHIFT] = x32[0:SHIFT].astype(BF)
    out[SHIFT : LAT - SHIFT] = done[...]
    out[LAT - SHIFT : LAT] = x32[SHIFT : 2 * SHIFT].astype(BF)


def work_space(counts):
    total, asked = KEYS * len(counts), sum(counts)
    return [
        pltpu.VMEM((total, WIDTH), F32),
        pltpu.VMEM((total, WIDTH), BF),
        pltpu.VMEM((asked, WIDTH), BF),
        pltpu.VMEM((total, 2 * WIDTH), BF),
        pltpu.VMEM((asked, WIDTH), BF),
        pltpu.VMEM((asked, WIDTH), BF),
        pltpu.VMEM((asked, WIDTH), F32),
    ]


def call(body, out_shape, scratch, flops, *operands, smem=0):
    vmem = pl.BlockSpec(memory_space=pltpu.VMEM)
    specs = [pl.BlockSpec(memory_space=pltpu.SMEM)] * smem + [vmem] * (len(operands) - smem)
    return pl.pallas_call(
        body,
        out_shape=out_shape,
        in_specs=specs,
        out_specs=jax.tree.map(lambda _: vmem, out_shape),
        scratch_shapes=scratch,
        compiler_params=pltpu.CompilerParams(vmem_limit_bytes=40 * 2**20),
        cost_estimate=pl.CostEstimate(flops=flops, bytes_accessed=4_000_000, transcendentals=0),
    )(*operands)


def shards(tokens, norm_gain, w_qkv, w_out, pole_mask):
    x = jnp.transpose(tokens, (1, 0, 2))
    gain = norm_gain.reshape(1, WIDTH)
    lons, lats = lax.axis_size("lon"), lax.axis_size("lat")
    eastward = [(i, (i + 1) % lons) for i in range(lons)]
    northward = [(i, i + 1) for i in range(lats - 1)]
    edge = jax.ShapeDtypeStruct((EDGE, WIDTH), BF)
    inner = jax.ShapeDtypeStruct((LAT - 2 * SHIFT, LON, WIDTH), BF)
    edge32 = pltpu.VMEM((EDGE, WIDTH), F32)
    inner32 = pltpu.VMEM((LAT - 2 * SHIFT, LON, WIDTH), F32)
    east, west = call(pack_lon, (edge, edge), [edge32, edge32], 1_000_000, x)
    from_west = lax.ppermute(east, "lon", eastward)
    from_east = lax.ppermute(west, "lon", [(b, a) for a, b in eastward])
    part = call(middle, inner, [inner32] + work_space((144, 144)), 2_000_000_000, x, gain, w_qkv, w_out)
    north, south = call(pack_lat, (edge, edge), [pltpu.VMEM((72, WIDTH), F32)], 1_000_000, x, from_west, from_east)
    from_south = lax.ppermute(north, "lat", northward)
    from_north = lax.ppermute(south, "lat", [(b, a) for a, b in northward])
    part = call(
        sides, inner, [inner32, edge32, edge32] + work_space((80,) * 4), 2_000_000_000,
        x, from_west, from_east, part, gain, w_qkv, w_out,
    )
    poles32 = pltpu.VMEM((2 * SHIFT, LON, WIDTH), F32)
    mixed = call(
        poles, jax.ShapeDtypeStruct((LAT, LON, WIDTH), BF),
        [poles32] + [edge32] * 4 + work_space((80, 48, 48) * 2), 2_000_000_000,
        pole_mask, x, from_west, from_east, from_south, from_north, part, gain, w_qkv, w_out, smem=1,
    )
    return jnp.transpose(mixed, (1, 0, 2))


def solution(mesh):
    in_specs = (P("lon", "lat", None), P(), P(), P(), P())
    out_specs = P("lon", "lat", None)
    return jax.shard_map(shards, mesh=mesh, in_specs=in_specs, out_specs=out_specs, check_vma=False)
```

```python
import functools

import jax
import jax.numpy as jnp
from jax import lax
from jax.experimental import pallas as pl
from jax.experimental.pallas import tpu as pltpu
from jax.sharding import PartitionSpec as P

WIDTH = 512
HEADS = 8
WINDOW = 12
SHIFT = 6
KEYS = WINDOW * WINDOW
EPS = 1e-05
NLAT = 288
LON = 24
LAT = 36
EDGE = LAT * SHIFT
HALF = 80
BF = jnp.bfloat16
F32 = jnp.float32


def normalise(window_tokens, gain, normed, block):
    for start in range(0, normed.shape[0], block):
        values = window_tokens[start : start + block, :].astype(F32)
        average = jnp.sum(values, axis=-1, keepdims=True) * (1.0 / WIDTH)
        centred = values - average
        variance = jnp.sum(centred * centred, axis=-1, keepdims=True) * (1.0 / WIDTH)
        normed[start : start + block, :] = (centred * lax.rsqrt(variance + EPS) * gain).astype(BF)


def project_pairs(normed, w_qkv, pairs):
    for col in range(0, 2 * WIDTH, 256):
        part = jnp.dot(normed[...], w_qkv[:, WIDTH + col : WIDTH + col + 256], preferred_element_type=F32)
        pairs[:, col : col + 256] = part.astype(BF)


def project_queries(rows, w_qkv, queries):
    for col in range(0, WIDTH, 256):
        part = jnp.dot(rows[...], w_qkv[:, col : col + 256], preferred_element_type=F32)
        queries[:, col : col + 256] = (part.astype(BF).astype(F32) * (WIDTH // HEADS) ** (-0.5)).astype(BF)


def window_context(queries, q_base, count, key_parts, context, bias):
    lane = lax.broadcasted_iota(jnp.int32, (1, 128), 1)
    low32 = lane < 64
    keep_low = low32.astype(F32).astype(BF)
    keep_high = (lane >= 64).astype(F32).astype(BF)
    ones = jnp.ones((sum(part[2] for part in key_parts), 128), BF)

    def rows_of(col):
        found = [ref[base : base + rows, col : col + 128] for ref, base, rows in key_parts]
        return found[0] if len(found) == 1 else jnp.concatenate(found, axis=0)

    for pair in range(HEADS // 2):
        cols = slice(128 * pair, 128 * pair + 128)
        both = queries[q_base : q_base + count, cols]
        stacked = jnp.concatenate([both * keep_low, both * keep_high], axis=0)
        key_part, value_part = rows_of(128 * pair), rows_of(WIDTH + 128 * pair)
        scores = lax.dot_general(stacked, key_part, (((1,), (1,)), ((), ())), preferred_element_type=F32)
        if bias is not None:
            scores = scores + bias
        row_max = jnp.max(scores, axis=-1, keepdims=True)
        exp_scores = jnp.exp(scores - row_max).astype(BF)
        widened = jnp.concatenate([value_part, ones], axis=1)
        summed = jnp.dot(exp_scores, widened, preferred_element_type=F32)
        first, second = summed[:count], summed[count:]
        top = jnp.where(low32, first[:, :128], second[:, :128])
        under = jnp.where(low32, first[:, 128:], second[:, 128:])
        context[q_base : q_base + count, cols] = (top / under).astype(BF)


def finish(context, w_out, residual, stride, count, mixed):
    for col in range(0, WIDTH, 256):
        part = jnp.dot(context[...], w_out[:, col : col + 256], preferred_element_type=F32)
        for index in range(mixed.shape[0] // count):
            here = slice(count * index, count * index + count)
            own = residual[stride * index : stride * index + count, col : col + 256].astype(F32)
            mixed[here, col : col + 256] = part[here] + own


def attend(window_tokens, gain_ref, w_qkv, w_out, count, normed, q_rows, pairs, queries, context, mixed):
    windows = normed.shape[0] // KEYS
    normalise(window_tokens, gain_ref[...], normed, KEYS)
    for index in range(windows):
        q_rows[count * index : count * index + count, :] = normed[KEYS * index : KEYS * index + count, :]
    project_pairs(normed, w_qkv, pairs)
    project_queries(q_rows, w_qkv, queries)
    for index in range(windows):
        window_context(queries, count * index, count, [(pairs, KEYS * index, KEYS)], context, None)
    finish(context, w_out, window_tokens, KEYS, count, mixed)


def pack_lon(x, east, west, east32, west32):
    for lat in range(LAT):
        row = x[lat].astype(F32)
        west32[SHIFT * lat : SHIFT * lat + SHIFT, :] = row[0:SHIFT]
        east32[SHIFT * lat : SHIFT * lat + SHIFT, :] = row[LON - SHIFT : LON]
    west[...] = west32[...].astype(BF)
    east[...] = east32[...].astype(BF)


def pack_lat(x, from_west, from_east, north, south, work):
    own = SHIFT * LON
    for target, lat, halo in ((south, 0, 0), (north, LAT - SHIFT, EDGE - 36)):
        target[0:own, :] = x[lat : lat + SHIFT].reshape(own, WIDTH)
        work[0:36, :] = from_west[...].astype(F32)[halo : halo + 36]
        work[36:72, :] = from_east[...].astype(F32)[halo : halo + 36]
        target[own : own + 72, :] = work[...].astype(BF)


def middle(x, gain, w_qkv, w_out, out, x32, stack, normed, q_rows, pairs, queries, context, mixed):
    x32[...] = x[SHIFT : LAT - SHIFT].astype(F32)
    for lat in range(24):
        stack[12 * lat : 12 * lat + 12, :] = x32[lat, 6:18, :]
    attend(stack, gain, w_qkv, w_out, KEYS, normed, q_rows, pairs, queries, context, mixed)
    for lat in range(24):
        x32[lat, 6:18, :] = mixed[12 * lat : 12 * lat + 12, :]
    out[...] = x32[...].astype(BF)


def sides(x, from_west, from_east, done, gain, w_qkv, w_out, out, x32, w32, e32, stack, normed, q_rows, pairs, queries, context, mixed):
    x32[...] = x[SHIFT : LAT - SHIFT].astype(F32)
    w32[...] = from_west[...].astype(F32)
    e32[...] = from_east[...].astype(F32)
    for index in range(4):
        band, east = index // 2, index % 2
        lon = 18 if east else 0
        base = KEYS * index
        for step in range(12):
            stack[base + 6 * step : base + 6 * step + 6, :] = x32[12 * band + step, lon : lon + 6, :]
        halo = e32 if east else w32
        stack[base + 72 : base + 144, :] = halo[36 + 72 * band : 108 + 72 * band, :]
    attend(stack, gain, w_qkv, w_out, HALF, normed, q_rows, pairs, queries, context, mixed)
    x32[...] = done[...].astype(F32)
    for index in range(4):
        band, east = index // 2, index % 2
        lon = 18 if east else 0
        for step in range(12):
            x32[12 * band + step, lon : lon + 6, :] = mixed[HALF * index + 6 * step : HALF * index + 6 * step + 6, :]
    out[...] = x32[...].astype(BF)


def prepare(x, from_west, from_east, gain, w_qkv, raw, queries, pairs, x32, w32, e32, stack, normed):
    x32[0:SHIFT] = x[0:SHIFT].astype(F32)
    x32[SHIFT : 2 * SHIFT] = x[LAT - SHIFT : LAT].astype(F32)
    w32[...] = from_west[...].astype(F32)
    e32[...] = from_east[...].astype(F32)
    for north in range(2):
        base = 3 * HALF * north
        for step in range(SHIFT):
            at = SHIFT * north + step
            stack[base + 12 * step : base + 12 * step + 12, :] = x32[at, 6:18, :]
            stack[base + 80 + 6 * step : base + 86 + 6 * step, :] = x32[at, 0:6, :]
            stack[base + 160 + 6 * step : base + 166 + 6 * step, :] = x32[at, 18:24, :]
        halo = EDGE - 36 if north else 0
        stack[base + 116 : base + 152, :] = w32[halo : halo + 36, :]
        stack[base + 196 : base + 232, :] = e32[halo : halo + 36, :]
        for window in range(3):
            stack[base + 80 * window + 72 : base + 80 * window + 80, :] = jnp.zeros((8, WIDTH), F32)
    raw[...] = stack[...].astype(BF)
    normalise(raw, gain[...], normed, HALF)
    project_pairs(normed, w_qkv, pairs)
    project_queries(normed, w_qkv, queries)


def pole_bias(mask, band, north):
    key = lax.broadcasted_iota(jnp.int32, (1, 2 * HALF), 1)
    in_halo = key >= HALF
    inner = jnp.where(in_halo, key - HALF, key)
    row_wide = inner // 12
    row_corner = jnp.where(inner >= 36, inner - 36, inner) // 6
    real = inner < 72
    bias_wide = jnp.full((1, 2 * HALF), -1e30, F32)
    bias_corner = bias_wide
    lat_at = band * LAT + (LAT - SHIFT if north else 0)
    halo_at = band * LAT + (LAT if north else -SHIFT)
    for step in range(SHIFT):
        there = halo_at + step
        exists = jnp.logical_and(there >= 0, there < NLAT)
        halo_ok = jnp.logical_and(exists, mask[jnp.clip(there, 0, NLAT - 1)] == 1)
        own_bias = jnp.where(mask[lat_at + step] == 1, 0.0, -1e30)
        halo_bias = jnp.where(halo_ok, 0.0, -1e30)
        step_bias = jnp.where(in_halo, halo_bias, own_bias)
        bias_wide = jnp.where(jnp.logical_and(real, row_wide == step), step_bias, bias_wide)
        bias_corner = jnp.where(jnp.logical_and(real, row_corner == step), step_bias, bias_corner)
    return bias_wide, bias_corner


def poles(
    mask, raw, queries, own_pairs, from_south, from_north, done, gain, w_qkv, w_out, out,
    s32, n32, stack, normed, pairs, context, mixed, x32, rows, sem,
):
    inner_copy = pltpu.make_async_copy(done, out.at[SHIFT : LAT - SHIFT], sem.at[0])
    inner_copy.start()
    s32[...] = from_south[...].astype(F32)
    n32[...] = from_north[...].astype(F32)
    band = lax.axis_index("lat")
    biases = []
    for north in range(2):
        halo = n32 if north else s32
        base = 3 * HALF * north
        for step in range(SHIFT):
            at = LON * step
            stack[base + 12 * step : base + 12 * step + 12, :] = halo[at + 6 : at + 18, :]
            stack[base + 80 + 6 * step : base + 86 + 6 * step, :] = halo[at : at + 6, :]
            stack[base + 160 + 6 * step : base + 166 + 6 * step, :] = halo[at + 18 : at + 24, :]
        stack[base + 116 : base + 152, :] = halo[144:180, :]
        stack[base + 196 : base + 232, :] = halo[180:216, :]
        for window in range(3):
            stack[base + 80 * window + 72 : base + 80 * window + 80, :] = jnp.zeros((8, WIDTH), F32)
        wide, corner = pole_bias(mask, band, north)
        biases += [wide, corner, corner]
    normalise(stack, gain[...], normed, HALF)
    project_pairs(normed, w_qkv, pairs)
    for index in range(6):
        at = HALF * index
        window_context(queries, at, HALF, [(own_pairs, at, HALF), (pairs, at, HALF)], context, biases[index])
    finish(context, w_out, raw, HALF, HALF, mixed)
    for north in range(2):
        base = 3 * HALF * north
        for step in range(SHIFT):
            at = SHIFT * north + step
            x32[at, 6:18, :] = mixed[base + 12 * step : base + 12 * step + 12, :]
            x32[at, 0:6, :] = mixed[base + 80 + 6 * step : base + 86 + 6 * step, :]
            x32[at, 18:24, :] = mixed[base + 160 + 6 * step : base + 166 + 6 * step, :]
    rows[...] = x32[...].astype(BF)
    south_copy = pltpu.make_async_copy(rows.at[0:SHIFT], out.at[0:SHIFT], sem.at[1])
    north_copy = pltpu.make_async_copy(rows.at[SHIFT : 2 * SHIFT], out.at[LAT - SHIFT : LAT], sem.at[2])
    south_copy.start()
    north_copy.start()
    inner_copy.wait()
    south_copy.wait()
    north_copy.wait()


def vmem(rows, columns=WIDTH, dtype=BF):
    return pltpu.VMEM((rows, columns), dtype)


def work_space(windows, count):
    total, asked = KEYS * windows, count * windows
    return [
        vmem(total, dtype=F32), vmem(total), vmem(asked), vmem(total, 2 * WIDTH),
        vmem(asked), vmem(asked), vmem(asked, dtype=F32),
    ]


def call(body, out_shape, scratch, flops, *operands, smem=0, in_hbm=False):
    whole = pl.BlockSpec(memory_space=pltpu.VMEM)
    out_spec = pl.BlockSpec(memory_space=pl.ANY) if in_hbm else whole
    specs = [pl.BlockSpec(memory_space=pltpu.SMEM)] * smem + [whole] * (len(operands) - smem)
    return pl.pallas_call(
        body,
        out_shape=out_shape,
        in_specs=specs,
        out_specs=jax.tree.map(lambda _: out_spec, out_shape),
        scratch_shapes=scratch,
        compiler_params=pltpu.CompilerParams(vmem_limit_bytes=40 * 2**20),
        cost_estimate=pl.CostEstimate(flops=flops, bytes_accessed=4_000_000, transcendentals=0),
    )(*operands)


def shards(tokens, norm_gain, w_qkv, w_out, pole_mask):
    x = jnp.transpose(tokens, (1, 0, 2))
    gain = norm_gain.reshape(1, WIDTH)
    lons, lats = lax.axis_size("lon"), lax.axis_size("lat")
    eastward = [(i, (i + 1) % lons) for i in range(lons)]
    northward = [(i, i + 1) for i in range(lats - 1)]
    edge = jax.ShapeDtypeStruct((EDGE, WIDTH), BF)
    inner = jax.ShapeDtypeStruct((LAT - 2 * SHIFT, LON, WIDTH), BF)
    edge32 = vmem(EDGE, dtype=F32)
    inner32 = pltpu.VMEM((LAT - 2 * SHIFT, LON, WIDTH), F32)
    poles32 = pltpu.VMEM((2 * SHIFT, LON, WIDTH), F32)
    east, west = call(pack_lon, (edge, edge), [edge32, edge32], 8_000_000_000, x)
    from_west = lax.ppermute(east, "lon", eastward)
    from_east = lax.ppermute(west, "lon", [(b, a) for a, b in eastward])
    part = call(middle, inner, [inner32] + work_space(2, KEYS), 2_000_000_000, x, gain, w_qkv, w_out)
    part, from_west, from_east = lax.optimization_barrier((part, from_west, from_east))
    north, south = call(pack_lat, (edge, edge), [vmem(72, dtype=F32)], 1_000_000, x, from_west, from_east)
    from_south = lax.ppermute(north, "lat", northward)
    from_north = lax.ppermute(south, "lat", [(b, a) for a, b in northward])
    part = call(
        sides, inner, [inner32, edge32, edge32] + work_space(4, HALF), 2_000_000_000,
        x, from_west, from_east, part, gain, w_qkv, w_out,
    )
    rows = 6 * HALF
    raw, queries, pairs = call(
        prepare, tuple(jax.ShapeDtypeStruct((rows, n), BF) for n in (WIDTH, WIDTH, 2 * WIDTH)),
        [poles32, edge32, edge32, vmem(rows, dtype=F32), vmem(rows)], 2_000_000_000,
        x, from_west, from_east, gain, w_qkv,
    )
    mixed = call(
        poles, jax.ShapeDtypeStruct((LAT, LON, WIDTH), BF),
        [
            edge32, edge32, vmem(rows, dtype=F32), vmem(rows), vmem(rows, 2 * WIDTH), vmem(rows), vmem(rows, dtype=F32),
            poles32, pltpu.VMEM((2 * SHIFT, LON, WIDTH), BF), pltpu.SemaphoreType.DMA((3,)),
        ], 2_000_000_000,
        pole_mask, raw, queries, pairs, from_south, from_north, part, gain, w_qkv, w_out, smem=1, in_hbm=True,
    )
    return jnp.transpose(mixed, (1, 0, 2))


def solution(mesh):
    in_specs = (P("lon", "lat", None), P(), P(), P(), P())
    out_specs = P("lon", "lat", None)
    return jax.shard_map(shards, mesh=mesh, in_specs=in_specs, out_specs=out_specs, check_vma=False)
```

```python
import functools

import jax
import jax.numpy as jnp
from jax import lax
from jax.experimental import pallas as pl
from jax.experimental.pallas import tpu as pltpu
from jax.sharding import PartitionSpec as P

WIDTH = 512
HEADS = 8
WINDOW = 12
SHIFT = 6
KEYS = WINDOW * WINDOW
EPS = 1e-05
NLAT = 288
LON = 24
LAT = 36
EDGE = LAT * SHIFT
HALF = 80
BF = jnp.bfloat16
F32 = jnp.float32


def normalise(window_tokens, gain, normed, block):
    for start in range(0, normed.shape[0], block):
        values = window_tokens[start : start + block, :].astype(F32)
        average = jnp.sum(values, axis=-1, keepdims=True) * (1.0 / WIDTH)
        centred = values - average
        variance = jnp.sum(centred * centred, axis=-1, keepdims=True) * (1.0 / WIDTH)
        normed[start : start + block, :] = (centred * lax.rsqrt(variance + EPS) * gain).astype(BF)


def project_pairs(normed, w_qkv, pairs):
    for col in range(0, 2 * WIDTH, 256):
        part = jnp.dot(normed[...], w_qkv[:, WIDTH + col : WIDTH + col + 256], preferred_element_type=F32)
        pairs[:, col : col + 256] = part.astype(BF)


def project_queries(rows, w_qkv, queries):
    for col in range(0, WIDTH, 256):
        part = jnp.dot(rows[...], w_qkv[:, col : col + 256], preferred_element_type=F32)
        queries[:, col : col + 256] = (part.astype(BF).astype(F32) * (WIDTH // HEADS) ** (-0.5)).astype(BF)


def window_context(queries, q_base, c_base, count, key_parts, context, bias):
    lane = lax.broadcasted_iota(jnp.int32, (1, 128), 1)
    low32 = lane < 64
    keep_low = low32.astype(F32).astype(BF)
    keep_high = (lane >= 64).astype(F32).astype(BF)
    ones = jnp.ones((sum(part[2] for part in key_parts), 128), BF)

    def rows_of(col):
        found = [ref[base : base + rows, col : col + 128] for ref, base, rows in key_parts]
        return found[0] if len(found) == 1 else jnp.concatenate(found, axis=0)

    for pair in range(HEADS // 2):
        cols = slice(128 * pair, 128 * pair + 128)
        both = queries[q_base : q_base + count, cols]
        stacked = jnp.concatenate([both * keep_low, both * keep_high], axis=0)
        key_part, value_part = rows_of(128 * pair), rows_of(WIDTH + 128 * pair)
        scores = lax.dot_general(stacked, key_part, (((1,), (1,)), ((), ())), preferred_element_type=F32)
        if bias is not None:
            scores = scores + bias
        row_max = jnp.max(scores, axis=-1, keepdims=True)
        exp_scores = jnp.exp(scores - row_max).astype(BF)
        widened = jnp.concatenate([value_part, ones], axis=1)
        summed = jnp.dot(exp_scores, widened, preferred_element_type=F32)
        first, second = summed[:count], summed[count:]
        top = jnp.where(low32, first[:, :128], second[:, :128])
        under = jnp.where(low32, first[:, 128:], second[:, 128:])
        context[c_base : c_base + count, cols] = (top / under).astype(BF)


def finish(context, w_out, residual, base, stride, count, mixed):
    for col in range(0, WIDTH, 256):
        part = jnp.dot(context[...], w_out[:, col : col + 256], preferred_element_type=F32)
        for index in range(mixed.shape[0] // count):
            here = slice(count * index, count * index + count)
            own = residual[base + stride * index : base + stride * index + count, col : col + 256].astype(F32)
            mixed[here, col : col + 256] = part[here] + own


def attend(window_tokens, gain_ref, w_qkv, w_out, count, normed, q_rows, pairs, queries, context, mixed):
    windows = normed.shape[0] // KEYS
    normalise(window_tokens, gain_ref[...], normed, KEYS)
    for index in range(windows):
        q_rows[count * index : count * index + count, :] = normed[KEYS * index : KEYS * index + count, :]
    project_pairs(normed, w_qkv, pairs)
    project_queries(q_rows, w_qkv, queries)
    for index in range(windows):
        window_context(queries, count * index, count * index, count, [(pairs, KEYS * index, KEYS)], context, None)
    finish(context, w_out, window_tokens, 0, KEYS, count, mixed)


def pack_lon(x, east, west, east32, west32):
    for lat in range(LAT):
        row = x[lat].astype(F32)
        west32[SHIFT * lat : SHIFT * lat + SHIFT, :] = row[0:SHIFT]
        east32[SHIFT * lat : SHIFT * lat + SHIFT, :] = row[LON - SHIFT : LON]
    west[...] = west32[...].astype(BF)
    east[...] = east32[...].astype(BF)


def pack_lat(x, from_west, from_east, north, south, work):
    own = SHIFT * LON
    for target, lat, halo in ((south, 0, 0), (north, LAT - SHIFT, EDGE - 36)):
        target[0:own, :] = x[lat : lat + SHIFT].reshape(own, WIDTH)
        work[0:36, :] = from_west[...].astype(F32)[halo : halo + 36]
        work[36:72, :] = from_east[...].astype(F32)[halo : halo + 36]
        target[own : own + 72, :] = work[...].astype(BF)


def middle(x, gain, w_qkv, w_out, out, x32, stack, normed, q_rows, pairs, queries, context, mixed):
    x32[...] = x[SHIFT : LAT - SHIFT].astype(F32)
    for lat in range(24):
        stack[12 * lat : 12 * lat + 12, :] = x32[lat, 6:18, :]
    attend(stack, gain, w_qkv, w_out, KEYS, normed, q_rows, pairs, queries, context, mixed)
    for lat in range(24):
        x32[lat, 6:18, :] = mixed[12 * lat : 12 * lat + 12, :]
    out[...] = x32[...].astype(BF)


def side_windows(east, x, halo, done, gain, w_qkv, w_out, out, x32, halo32, stack, normed, q_rows, pairs, queries, context, mixed):
    lon = LON - SHIFT if east else 0
    x32[...] = x[SHIFT : LAT - SHIFT].astype(F32)
    halo32[...] = halo[...].astype(F32)
    for band in range(2):
        base = KEYS * band
        for step in range(12):
            stack[base + 6 * step : base + 6 * step + 6, :] = x32[12 * band + step, lon : lon + 6, :]
        stack[base + 72 : base + 144, :] = halo32[36 + 72 * band : 108 + 72 * band, :]
    attend(stack, gain, w_qkv, w_out, HALF, normed, q_rows, pairs, queries, context, mixed)
    x32[...] = done[...].astype(F32)
    for band in range(2):
        for step in range(12):
            x32[12 * band + step, lon : lon + 6, :] = mixed[HALF * band + 6 * step : HALF * band + 6 * step + 6, :]
    out[...] = x32[...].astype(BF)


def west_side(*refs):
    side_windows(False, *refs)


def east_side(*refs):
    side_windows(True, *refs)


def prepare(x, from_west, from_east, gain, w_qkv, raw, queries, pairs, x32, w32, e32, stack, normed):
    x32[0:SHIFT] = x[0:SHIFT].astype(F32)
    x32[SHIFT : 2 * SHIFT] = x[LAT - SHIFT : LAT].astype(F32)
    w32[...] = from_west[...].astype(F32)
    e32[...] = from_east[...].astype(F32)
    for north in range(2):
        base = 3 * HALF * north
        for step in range(SHIFT):
            at = SHIFT * north + step
            stack[base + 12 * step : base + 12 * step + 12, :] = x32[at, 6:18, :]
            stack[base + 80 + 6 * step : base + 86 + 6 * step, :] = x32[at, 0:6, :]
            stack[base + 160 + 6 * step : base + 166 + 6 * step, :] = x32[at, 18:24, :]
        halo = EDGE - 36 if north else 0
        stack[base + 116 : base + 152, :] = w32[halo : halo + 36, :]
        stack[base + 196 : base + 232, :] = e32[halo : halo + 36, :]
        for window in range(3):
            stack[base + 80 * window + 72 : base + 80 * window + 80, :] = jnp.zeros((8, WIDTH), F32)
    raw[...] = stack[...].astype(BF)
    normalise(raw, gain[...], normed, HALF)
    project_pairs(normed, w_qkv, pairs)
    project_queries(normed, w_qkv, queries)


def pole_bias(mask, band, north):
    key = lax.broadcasted_iota(jnp.int32, (1, 2 * HALF), 1)
    in_halo = key >= HALF
    inner = jnp.where(in_halo, key - HALF, key)
    row_wide = inner // 12
    row_corner = jnp.where(inner >= 36, inner - 36, inner) // 6
    real = inner < 72
    bias_wide = jnp.full((1, 2 * HALF), -1e30, F32)
    bias_corner = bias_wide
    lat_at = band * LAT + (LAT - SHIFT if north else 0)
    halo_at = band * LAT + (LAT if north else -SHIFT)
    for step in range(SHIFT):
        there = halo_at + step
        exists = jnp.logical_and(there >= 0, there < NLAT)
        halo_ok = jnp.logical_and(exists, mask[jnp.clip(there, 0, NLAT - 1)] == 1)
        own_bias = jnp.where(mask[lat_at + step] == 1, 0.0, -1e30)
        halo_bias = jnp.where(halo_ok, 0.0, -1e30)
        step_bias = jnp.where(in_halo, halo_bias, own_bias)
        bias_wide = jnp.where(jnp.logical_and(real, row_wide == step), step_bias, bias_wide)
        bias_corner = jnp.where(jnp.logical_and(real, row_corner == step), step_bias, bias_corner)
    return bias_wide, bias_corner


def pole_windows(
    north, mask, raw, queries, own_pairs, arrived, gain, w_qkv, w_out, result,
    halo, stack, normed, pairs, context, mixed, x32,
):
    halo[...] = arrived[...].astype(F32)
    for step in range(SHIFT):
        at = LON * step
        stack[12 * step : 12 * step + 12, :] = halo[at + 6 : at + 18, :]
        stack[80 + 6 * step : 86 + 6 * step, :] = halo[at : at + 6, :]
        stack[160 + 6 * step : 166 + 6 * step, :] = halo[at + 18 : at + 24, :]
    stack[116:152, :] = halo[144:180, :]
    stack[196:232, :] = halo[180:216, :]
    for window in range(3):
        stack[80 * window + 72 : 80 * window + 80, :] = jnp.zeros((8, WIDTH), F32)
    wide, corner = pole_bias(mask, lax.axis_index("lat"), north)
    normalise(stack, gain[...], normed, HALF)
    project_pairs(normed, w_qkv, pairs)
    base = 3 * HALF * north
    for index, bias in enumerate((wide, corner, corner)):
        at = HALF * index
        parts = [(own_pairs, base + at, HALF), (pairs, at, HALF)]
        window_context(queries, base + at, at, HALF, parts, context, bias)
    finish(context, w_out, raw, base, HALF, HALF, mixed)
    for step in range(SHIFT):
        x32[step, 6:18, :] = mixed[12 * step : 12 * step + 12, :]
        x32[step, 0:6, :] = mixed[80 + 6 * step : 86 + 6 * step, :]
        x32[step, 18:24, :] = mixed[160 + 6 * step : 166 + 6 * step, :]
    result[...] = x32[...].astype(BF)


def south_pole(*refs):
    pole_windows(0, *refs)


def north_pole(mask, raw, queries, own_pairs, arrived, inner, south, gain, w_qkv, w_out, out, *scratch):
    *work, rows, sem = scratch
    copies = [
        pltpu.make_async_copy(inner, out.at[SHIFT : LAT - SHIFT], sem.at[0]),
        pltpu.make_async_copy(south, out.at[0:SHIFT], sem.at[1]),
        pltpu.make_async_copy(rows, out.at[LAT - SHIFT : LAT], sem.at[2]),
    ]
    copies[0].start()
    copies[1].start()
    pole_windows(1, mask, raw, queries, own_pairs, arrived, gain, w_qkv, w_out, rows, *work)
    copies[2].start()
    for copy in copies:
        copy.wait()


def vmem(rows, columns=WIDTH, dtype=BF):
    return pltpu.VMEM((rows, columns), dtype)


def work_space(windows, count):
    total, asked = KEYS * windows, count * windows
    return [
        vmem(total, dtype=F32), vmem(total), vmem(asked), vmem(total, 2 * WIDTH),
        vmem(asked), vmem(asked), vmem(asked, dtype=F32),
    ]


def call(body, out_shape, scratch, flops, *operands, smem=0, in_hbm=False):
    whole = pl.BlockSpec(memory_space=pltpu.VMEM)
    out_spec = pl.BlockSpec(memory_space=pl.ANY) if in_hbm else whole
    specs = [pl.BlockSpec(memory_space=pltpu.SMEM)] * smem + [whole] * (len(operands) - smem)
    return pl.pallas_call(
        body,
        out_shape=out_shape,
        in_specs=specs,
        out_specs=jax.tree.map(lambda _: out_spec, out_shape),
        scratch_shapes=scratch,
        compiler_params=pltpu.CompilerParams(vmem_limit_bytes=40 * 2**20),
        cost_estimate=pl.CostEstimate(flops=flops, bytes_accessed=flops // 1000, transcendentals=0),
    )(*operands)


def shards(tokens, norm_gain, w_qkv, w_out, pole_mask):
    x = jnp.transpose(tokens, (1, 0, 2))
    gain = norm_gain.reshape(1, WIDTH)
    lons, lats = lax.axis_size("lon"), lax.axis_size("lat")
    eastward = [(i, (i + 1) % lons) for i in range(lons)]
    northward = [(i, i + 1) for i in range(lats - 1)]
    edge = jax.ShapeDtypeStruct((EDGE, WIDTH), BF)
    inner = jax.ShapeDtypeStruct((LAT - 2 * SHIFT, LON, WIDTH), BF)
    edge32 = vmem(EDGE, dtype=F32)
    inner32 = pltpu.VMEM((LAT - 2 * SHIFT, LON, WIDTH), F32)
    poles32 = pltpu.VMEM((2 * SHIFT, LON, WIDTH), F32)
    east, west = call(pack_lon, (edge, edge), [edge32, edge32], 8_000_000_000, x)
    from_west = lax.ppermute(east, "lon", eastward)
    from_east = lax.ppermute(west, "lon", [(b, a) for a, b in eastward])
    part = call(middle, inner, [inner32] + work_space(2, KEYS), 2_000_000_000, x, gain, w_qkv, w_out)
    part, from_west = lax.optimization_barrier((part, from_west))
    side_work = [inner32, edge32] + work_space(2, HALF)
    part = call(west_side, inner, side_work, 1_000_000, x, from_west, part, gain, w_qkv, w_out)
    part, from_west, from_east = lax.optimization_barrier((part, from_west, from_east))
    north, south = call(pack_lat, (edge, edge), [vmem(72, dtype=F32)], 1_000_000, x, from_west, from_east)
    from_south = lax.ppermute(north, "lat", northward)
    from_north = lax.ppermute(south, "lat", [(b, a) for a, b in northward])
    part = call(east_side, inner, side_work, 1_000_000, x, from_east, part, gain, w_qkv, w_out)
    rows = 6 * HALF
    raw, queries, pairs = call(
        prepare, tuple(jax.ShapeDtypeStruct((rows, n), BF) for n in (WIDTH, WIDTH, 2 * WIDTH)),
        [poles32, edge32, edge32, vmem(rows, dtype=F32), vmem(rows)], 1_000_000,
        x, from_west, from_east, gain, w_qkv,
    )
    half = rows // 2
    work = [edge32, vmem(half, dtype=F32), vmem(half), vmem(half, 2 * WIDTH), vmem(half), vmem(half, dtype=F32)]
    work.append(pltpu.VMEM((SHIFT, LON, WIDTH), F32))
    part, from_south = lax.optimization_barrier((part, from_south))
    low = call(
        south_pole, jax.ShapeDtypeStruct((SHIFT, LON, WIDTH), BF), work, 1_000_000,
        pole_mask, raw, queries, pairs, from_south, gain, w_qkv, w_out, smem=1,
    )
    low, from_north = lax.optimization_barrier((low, from_north))
    mixed = call(
        north_pole, jax.ShapeDtypeStruct((LAT, LON, WIDTH), BF),
        work + [pltpu.VMEM((SHIFT, LON, WIDTH), BF), pltpu.SemaphoreType.DMA((3,))], 2_000_000_000,
        pole_mask, raw, queries, pairs, from_north, part, low, gain, w_qkv, w_out, smem=1, in_hbm=True,
    )
    return jnp.transpose(mixed, (1, 0, 2))


def solution(mesh):
    in_specs = (P("lon", "lat", None), P(), P(), P(), P())
    out_specs = P("lon", "lat", None)
    return jax.shard_map(shards, mesh=mesh, in_specs=in_specs, out_specs=out_specs, check_vma=False)
```

```python
import functools

import jax
import jax.numpy as jnp
from jax import lax
from jax.experimental import pallas as pl
from jax.experimental.pallas import tpu as pltpu
from jax.sharding import PartitionSpec as P

WIDTH = 512
HEADS = 8
WINDOW = 12
SHIFT = 6
KEYS = WINDOW * WINDOW
EPS = 1e-05
NLAT = 288
LON = 24
LAT = 36
EDGE = LAT * SHIFT
HALF = 80
BF = jnp.bfloat16
F32 = jnp.float32


def normalise(window_tokens, gain, normed, block):
    for start in range(0, normed.shape[0], block):
        values = window_tokens[start : start + block, :].astype(F32)
        average = jnp.sum(values, axis=-1, keepdims=True) * (1.0 / WIDTH)
        centred = values - average
        variance = jnp.sum(centred * centred, axis=-1, keepdims=True) * (1.0 / WIDTH)
        normed[start : start + block, :] = (centred * lax.rsqrt(variance + EPS) * gain).astype(BF)


def project_pairs(normed, w_qkv, pairs):
    for col in range(0, 2 * WIDTH, 256):
        part = jnp.dot(normed[...], w_qkv[:, WIDTH + col : WIDTH + col + 256], preferred_element_type=F32)
        pairs[:, col : col + 256] = part.astype(BF)


def project_queries(rows, w_qkv, queries):
    for col in range(0, WIDTH, 256):
        part = jnp.dot(rows[...], w_qkv[:, col : col + 256], preferred_element_type=F32)
        queries[:, col : col + 256] = (part.astype(BF).astype(F32) * (WIDTH // HEADS) ** (-0.5)).astype(BF)


def window_context(queries, q_base, c_base, count, key_parts, context, bias):
    lane = lax.broadcasted_iota(jnp.int32, (1, 128), 1)
    low32 = lane < 64
    keep_low = low32.astype(F32).astype(BF)
    keep_high = (lane >= 64).astype(F32).astype(BF)
    ones = jnp.ones((sum(part[2] for part in key_parts), 128), BF)

    def rows_of(col):
        found = [ref[pl.ds(base, rows), col : col + 128] for ref, base, rows in key_parts]
        return found[0] if len(found) == 1 else jnp.concatenate(found, axis=0)

    for pair in range(HEADS // 2):
        cols = slice(128 * pair, 128 * pair + 128)
        both = queries[pl.ds(q_base, count), cols]
        stacked = jnp.concatenate([both * keep_low, both * keep_high], axis=0)
        key_part, value_part = rows_of(128 * pair), rows_of(WIDTH + 128 * pair)
        scores = lax.dot_general(stacked, key_part, (((1,), (1,)), ((), ())), preferred_element_type=F32)
        if bias is not None:
            scores = scores + bias
        row_max = jnp.max(scores, axis=-1, keepdims=True)
        exp_scores = jnp.exp(scores - row_max).astype(BF)
        widened = jnp.concatenate([value_part, ones], axis=1)
        summed = jnp.dot(exp_scores, widened, preferred_element_type=F32)
        first, second = summed[:count], summed[count:]
        top = jnp.where(low32, first[:, :128], second[:, :128])
        under = jnp.where(low32, first[:, 128:], second[:, 128:])
        context[c_base : c_base + count, cols] = (top / under).astype(BF)


def finish(context, w_out, residual, base, stride, count, mixed):
    for col in range(0, WIDTH, 256):
        part = jnp.dot(context[...], w_out[:, col : col + 256], preferred_element_type=F32)
        for index in range(mixed.shape[0] // count):
            here = slice(count * index, count * index + count)
            own = residual[pl.ds(base + stride * index, count), col : col + 256].astype(F32)
            mixed[here, col : col + 256] = part[here] + own


def attend(window_tokens, gain_ref, w_qkv, w_out, count, normed, q_rows, pairs, queries, context, mixed):
    windows = normed.shape[0] // KEYS
    normalise(window_tokens, gain_ref[...], normed, KEYS)
    for index in range(windows):
        q_rows[count * index : count * index + count, :] = normed[KEYS * index : KEYS * index + count, :]
    project_pairs(normed, w_qkv, pairs)
    project_queries(q_rows, w_qkv, queries)
    for index in range(windows):
        window_context(queries, count * index, count * index, count, [(pairs, KEYS * index, KEYS)], context, None)
    finish(context, w_out, window_tokens, 0, KEYS, count, mixed)


def pack_lon(x, east, west, east32, west32):
    for lat in range(LAT):
        row = x[lat].astype(F32)
        west32[SHIFT * lat : SHIFT * lat + SHIFT, :] = row[0:SHIFT]
        east32[SHIFT * lat : SHIFT * lat + SHIFT, :] = row[LON - SHIFT : LON]
    west[...] = west32[...].astype(BF)
    east[...] = east32[...].astype(BF)


def first_is_north():
    return 1 - lax.axis_index("lat") % 2


def pack_lat(x, from_west, from_east, first, second, work):
    own = SHIFT * LON

    def put(target, lat, halo):
        target[0:own, :] = x[lat : lat + SHIFT].reshape(own, WIDTH)
        work[0:36, :] = from_west[...].astype(F32)[halo : halo + 36]
        work[36:72, :] = from_east[...].astype(F32)[halo : halo + 36]
        target[own : own + 72, :] = work[...].astype(BF)

    @pl.when(first_is_north() == 1)
    def _():
        put(first, LAT - SHIFT, EDGE - 36)
        put(second, 0, 0)

    @pl.when(first_is_north() == 0)
    def _():
        put(first, 0, 0)
        put(second, LAT - SHIFT, EDGE - 36)


def middle(x, gain, w_qkv, w_out, out, x32, stack, normed, q_rows, pairs, queries, context, mixed):
    x32[...] = x[SHIFT : LAT - SHIFT].astype(F32)
    for lat in range(24):
        stack[12 * lat : 12 * lat + 12, :] = x32[lat, 6:18, :]
    attend(stack, gain, w_qkv, w_out, KEYS, normed, q_rows, pairs, queries, context, mixed)
    for lat in range(24):
        x32[lat, 6:18, :] = mixed[12 * lat : 12 * lat + 12, :]
    out[...] = x32[...].astype(BF)


def side_windows(east, x, halo, done, gain, w_qkv, w_out, out, x32, halo32, stack, normed, q_rows, pairs, queries, context, mixed):
    lon = LON - SHIFT if east else 0
    x32[...] = x[SHIFT : LAT - SHIFT].astype(F32)
    halo32[...] = halo[...].astype(F32)
    for band in range(2):
        base = KEYS * band
        for step in range(12):
            stack[base + 6 * step : base + 6 * step + 6, :] = x32[12 * band + step, lon : lon + 6, :]
        stack[base + 72 : base + 144, :] = halo32[36 + 72 * band : 108 + 72 * band, :]
    attend(stack, gain, w_qkv, w_out, HALF, normed, q_rows, pairs, queries, context, mixed)
    x32[...] = done[...].astype(F32)
    for band in range(2):
        for step in range(12):
            x32[12 * band + step, lon : lon + 6, :] = mixed[HALF * band + 6 * step : HALF * band + 6 * step + 6, :]
    out[...] = x32[...].astype(BF)


def west_side(*refs):
    side_windows(False, *refs)


def east_side(*refs):
    side_windows(True, *refs)


def prepare(x, from_west, from_east, gain, w_qkv, raw, queries, pairs, x32, w32, e32, stack, normed):
    x32[0:SHIFT] = x[0:SHIFT].astype(F32)
    x32[SHIFT : 2 * SHIFT] = x[LAT - SHIFT : LAT].astype(F32)
    w32[...] = from_west[...].astype(F32)
    e32[...] = from_east[...].astype(F32)
    for north in range(2):
        base = 3 * HALF * north
        for step in range(SHIFT):
            at = SHIFT * north + step
            stack[base + 12 * step : base + 12 * step + 12, :] = x32[at, 6:18, :]
            stack[base + 80 + 6 * step : base + 86 + 6 * step, :] = x32[at, 0:6, :]
            stack[base + 160 + 6 * step : base + 166 + 6 * step, :] = x32[at, 18:24, :]
        halo = EDGE - 36 if north else 0
        stack[base + 116 : base + 152, :] = w32[halo : halo + 36, :]
        stack[base + 196 : base + 232, :] = e32[halo : halo + 36, :]
        for window in range(3):
            stack[base + 80 * window + 72 : base + 80 * window + 80, :] = jnp.zeros((8, WIDTH), F32)
    raw[...] = stack[...].astype(BF)
    normalise(raw, gain[...], normed, HALF)
    project_pairs(normed, w_qkv, pairs)
    project_queries(normed, w_qkv, queries)


def pole_bias(mask, band, north):
    key = lax.broadcasted_iota(jnp.int32, (1, 2 * HALF), 1)
    in_halo = key >= HALF
    inner = jnp.where(in_halo, key - HALF, key)
    row_wide = inner // 12
    row_corner = jnp.where(inner >= 36, inner - 36, inner) // 6
    real = inner < 72
    bias_wide = jnp.full((1, 2 * HALF), -1e30, F32)
    bias_corner = bias_wide
    lat_at = band * LAT + (LAT - SHIFT) * north
    halo_at = band * LAT + (LAT + SHIFT) * north - SHIFT
    for step in range(SHIFT):
        there = halo_at + step
        exists = jnp.logical_and(there >= 0, there < NLAT)
        halo_ok = jnp.logical_and(exists, mask[jnp.clip(there, 0, NLAT - 1)] == 1)
        own_bias = jnp.where(mask[lat_at + step] == 1, 0.0, -1e30)
        halo_bias = jnp.where(halo_ok, 0.0, -1e30)
        step_bias = jnp.where(in_halo, halo_bias, own_bias)
        bias_wide = jnp.where(jnp.logical_and(real, row_wide == step), step_bias, bias_wide)
        bias_corner = jnp.where(jnp.logical_and(real, row_corner == step), step_bias, bias_corner)
    return bias_wide, bias_corner


def pole_windows(
    north, mask, raw, queries, own_pairs, arrived, gain, w_qkv, w_out, result,
    halo, stack, normed, pairs, context, mixed, x32,
):
    halo[...] = arrived[...].astype(F32)
    for step in range(SHIFT):
        at = LON * step
        stack[12 * step : 12 * step + 12, :] = halo[at + 6 : at + 18, :]
        stack[80 + 6 * step : 86 + 6 * step, :] = halo[at : at + 6, :]
        stack[160 + 6 * step : 166 + 6 * step, :] = halo[at + 18 : at + 24, :]
    stack[116:152, :] = halo[144:180, :]
    stack[196:232, :] = halo[180:216, :]
    for window in range(3):
        stack[80 * window + 72 : 80 * window + 80, :] = jnp.zeros((8, WIDTH), F32)
    wide, corner = pole_bias(mask, lax.axis_index("lat"), north)
    normalise(stack, gain[...], normed, HALF)
    project_pairs(normed, w_qkv, pairs)
    base = pl.multiple_of(3 * HALF * north, 3 * HALF)
    for index, bias in enumerate((wide, corner, corner)):
        at = HALF * index
        parts = [(own_pairs, base + at, HALF), (pairs, at, HALF)]
        window_context(queries, base + at, at, HALF, parts, context, bias)
    finish(context, w_out, raw, base, HALF, HALF, mixed)
    for step in range(SHIFT):
        x32[step, 6:18, :] = mixed[12 * step : 12 * step + 12, :]
        x32[step, 0:6, :] = mixed[80 + 6 * step : 86 + 6 * step, :]
        x32[step, 18:24, :] = mixed[160 + 6 * step : 166 + 6 * step, :]
    result[...] = x32[...].astype(BF)


def first_pole(*refs):
    pole_windows(first_is_north(), *refs)


def second_pole(mask, raw, queries, own_pairs, arrived, inner, early, gain, w_qkv, w_out, out, *scratch):
    *work, rows, sem = scratch
    north = 1 - first_is_north()
    far = LAT - SHIFT
    copies = [
        pltpu.make_async_copy(inner, out.at[SHIFT : LAT - SHIFT], sem.at[0]),
        pltpu.make_async_copy(early, out.at[pl.ds(far - far * north, SHIFT)], sem.at[1]),
        pltpu.make_async_copy(rows, out.at[pl.ds(far * north, SHIFT)], sem.at[2]),
    ]
    copies[0].start()
    copies[1].start()
    pole_windows(north, mask, raw, queries, own_pairs, arrived, gain, w_qkv, w_out, rows, *work)
    copies[2].start()
    for copy in copies:
        copy.wait()


def vmem(rows, columns=WIDTH, dtype=BF):
    return pltpu.VMEM((rows, columns), dtype)


def work_space(windows, count):
    total, asked = KEYS * windows, count * windows
    return [
        vmem(total, dtype=F32), vmem(total), vmem(asked), vmem(total, 2 * WIDTH),
        vmem(asked), vmem(asked), vmem(asked, dtype=F32),
    ]


def call(body, out_shape, scratch, flops, *operands, smem=0, in_hbm=False):
    whole = pl.BlockSpec(memory_space=pltpu.VMEM)
    out_spec = pl.BlockSpec(memory_space=pl.ANY) if in_hbm else whole
    specs = [pl.BlockSpec(memory_space=pltpu.SMEM)] * smem + [whole] * (len(operands) - smem)
    return pl.pallas_call(
        body,
        out_shape=out_shape,
        in_specs=specs,
        out_specs=jax.tree.map(lambda _: out_spec, out_shape),
        scratch_shapes=scratch,
        compiler_params=pltpu.CompilerParams(vmem_limit_bytes=40 * 2**20),
        cost_estimate=pl.CostEstimate(flops=flops, bytes_accessed=flops // 1000, transcendentals=0),
    )(*operands)


def shards(tokens, norm_gain, w_qkv, w_out, pole_mask):
    x = jnp.transpose(tokens, (1, 0, 2))
    gain = norm_gain.reshape(1, WIDTH)
    lons, lats = lax.axis_size("lon"), lax.axis_size("lat")
    eastward = [(i, (i + 1) % lons) for i in range(lons)]
    northward = [(i, i + 1) for i in range(lats - 1)]
    edge = jax.ShapeDtypeStruct((EDGE, WIDTH), BF)
    inner = jax.ShapeDtypeStruct((LAT - 2 * SHIFT, LON, WIDTH), BF)
    edge32 = vmem(EDGE, dtype=F32)
    inner32 = pltpu.VMEM((LAT - 2 * SHIFT, LON, WIDTH), F32)
    poles32 = pltpu.VMEM((2 * SHIFT, LON, WIDTH), F32)
    east, west = call(pack_lon, (edge, edge), [edge32, edge32], 8_000_000_000, x)
    from_west = lax.ppermute(east, "lon", eastward)
    from_east = lax.ppermute(west, "lon", [(b, a) for a, b in eastward])
    part = call(middle, inner, [inner32] + work_space(2, KEYS), 2_000_000_000, x, gain, w_qkv, w_out)
    part, from_west = lax.optimization_barrier((part, from_west))
    side_work = [inner32, edge32] + work_space(2, HALF)
    part = call(west_side, inner, side_work, 1_000_000, x, from_west, part, gain, w_qkv, w_out)
    part, from_west, from_east = lax.optimization_barrier((part, from_west, from_east))
    first, second = call(pack_lat, (edge, edge), [vmem(72, dtype=F32)], 1_000_000, x, from_west, from_east)
    met_first = lax.ppermute(first, "lat", [pair for a, b in northward[0::2] for pair in ((a, b), (b, a))])
    met_second = lax.ppermute(second, "lat", [pair for a, b in northward[1::2] for pair in ((a, b), (b, a))])
    part = call(east_side, inner, side_work, 1_000_000, x, from_east, part, gain, w_qkv, w_out)
    rows = 6 * HALF
    raw, queries, pairs = call(
        prepare, tuple(jax.ShapeDtypeStruct((rows, n), BF) for n in (WIDTH, WIDTH, 2 * WIDTH)),
        [poles32, edge32, edge32, vmem(rows, dtype=F32), vmem(rows)], 1_000_000,
        x, from_west, from_east, gain, w_qkv,
    )
    half = rows // 2
    work = [edge32, vmem(half, dtype=F32), vmem(half), vmem(half, 2 * WIDTH), vmem(half), vmem(half, dtype=F32)]
    work.append(pltpu.VMEM((SHIFT, LON, WIDTH), F32))
    part, met_first = lax.optimization_barrier((part, met_first))
    early = call(
        first_pole, jax.ShapeDtypeStruct((SHIFT, LON, WIDTH), BF), work, 1_000_000,
        pole_mask, raw, queries, pairs, met_first, gain, w_qkv, w_out, smem=1,
    )
    early, met_second = lax.optimization_barrier((early, met_second))
    mixed = call(
        second_pole, jax.ShapeDtypeStruct((LAT, LON, WIDTH), BF),
        work + [pltpu.VMEM((SHIFT, LON, WIDTH), BF), pltpu.SemaphoreType.DMA((3,))], 2_000_000_000,
        pole_mask, raw, queries, pairs, met_second, part, early, gain, w_qkv, w_out, smem=1, in_hbm=True,
    )
    return jnp.transpose(mixed, (1, 0, 2))


def solution(mesh):
    in_specs = (P("lon", "lat", None), P(), P(), P(), P())
    out_specs = P("lon", "lat", None)
    return jax.shard_map(shards, mesh=mesh, in_specs=in_specs, out_specs=out_specs, check_vma=False)
```

```python
import functools

import jax
import jax.numpy as jnp
from jax import lax
from jax.experimental import pallas as pl
from jax.experimental.pallas import tpu as pltpu
from jax.sharding import PartitionSpec as P

WIDTH = 512
HEADS = 8
WINDOW = 12
SHIFT = 6
KEYS = WINDOW * WINDOW
EPS = 1e-05
NLAT = 288
LON = 24
LAT = 36
EDGE = LAT * SHIFT
HALF = 80
BF = jnp.bfloat16
F32 = jnp.float32


def normalise(window_tokens, gain, normed, block):
    for start in range(0, normed.shape[0], block):
        values = window_tokens[start : start + block, :].astype(F32)
        average = jnp.sum(values, axis=-1, keepdims=True) * (1.0 / WIDTH)
        centred = values - average
        variance = jnp.sum(centred * centred, axis=-1, keepdims=True) * (1.0 / WIDTH)
        normed[start : start + block, :] = (centred * lax.rsqrt(variance + EPS) * gain).astype(BF)


def project_pairs(normed, w_qkv, pairs):
    for col in range(0, 2 * WIDTH, 256):
        part = jnp.dot(normed[...], w_qkv[:, WIDTH + col : WIDTH + col + 256], preferred_element_type=F32)
        pairs[:, col : col + 256] = part.astype(BF)


def project_queries(rows, w_qkv, queries):
    for col in range(0, WIDTH, 256):
        part = jnp.dot(rows[...], w_qkv[:, col : col + 256], preferred_element_type=F32)
        queries[:, col : col + 256] = (part.astype(BF).astype(F32) * (WIDTH // HEADS) ** (-0.5)).astype(BF)


def window_context(queries, q_base, c_base, count, key_parts, context, bias):
    lane = lax.broadcasted_iota(jnp.int32, (1, 128), 1)
    low32 = lane < 64
    keep_low = low32.astype(F32).astype(BF)
    keep_high = (lane >= 64).astype(F32).astype(BF)
    ones = jnp.ones((sum(part[2] for part in key_parts), 128), BF)

    def rows_of(col):
        found = [ref[pl.ds(base, rows), col : col + 128] for ref, base, rows in key_parts]
        return found[0] if len(found) == 1 else jnp.concatenate(found, axis=0)

    for pair in range(HEADS // 2):
        cols = slice(128 * pair, 128 * pair + 128)
        both = queries[pl.ds(q_base, count), cols]
        stacked = jnp.concatenate([both * keep_low, both * keep_high], axis=0)
        key_part, value_part = rows_of(128 * pair), rows_of(WIDTH + 128 * pair)
        scores = lax.dot_general(stacked, key_part, (((1,), (1,)), ((), ())), preferred_element_type=F32)
        if bias is not None:
            scores = scores + bias
        row_max = jnp.max(scores, axis=-1, keepdims=True)
        exp_scores = jnp.exp(scores - row_max).astype(BF)
        widened = jnp.concatenate([value_part, ones], axis=1)
        summed = jnp.dot(exp_scores, widened, preferred_element_type=F32)
        first, second = summed[:count], summed[count:]
        top = jnp.where(low32, first[:, :128], second[:, :128])
        under = jnp.where(low32, first[:, 128:], second[:, 128:])
        context[c_base : c_base + count, cols] = (top / under).astype(BF)


def finish(context, w_out, residual, base, stride, count, mixed):
    for col in range(0, WIDTH, 256):
        part = jnp.dot(context[...], w_out[:, col : col + 256], preferred_element_type=F32)
        for index in range(mixed.shape[0] // count):
            here = slice(count * index, count * index + count)
            own = residual[pl.ds(base + stride * index, count), col : col + 256].astype(F32)
            mixed[here, col : col + 256] = part[here] + own


def attend(window_tokens, gain_ref, w_qkv, w_out, count, normed, q_rows, pairs, queries, context, mixed):
    windows = normed.shape[0] // KEYS
    normalise(window_tokens, gain_ref[...], normed, KEYS)
    for index in range(windows):
        q_rows[count * index : count * index + count, :] = normed[KEYS * index : KEYS * index + count, :]
    project_pairs(normed, w_qkv, pairs)
    project_queries(q_rows, w_qkv, queries)
    for index in range(windows):
        window_context(queries, count * index, count * index, count, [(pairs, KEYS * index, KEYS)], context, None)
    finish(context, w_out, window_tokens, 0, KEYS, count, mixed)


def pack_lon(x, east, west, east32, west32):
    for lat in range(LAT):
        row = x[lat].astype(F32)
        west32[SHIFT * lat : SHIFT * lat + SHIFT, :] = row[0:SHIFT]
        east32[SHIFT * lat : SHIFT * lat + SHIFT, :] = row[LON - SHIFT : LON]
    west[...] = west32[...].astype(BF)
    east[...] = east32[...].astype(BF)


def first_is_north():
    return 1 - lax.axis_index("lat") % 2


def pack_lat(x, from_west, from_east, first, second, work):
    own = SHIFT * LON

    def put(target, lat, halo):
        target[0:own, :] = x[lat : lat + SHIFT].reshape(own, WIDTH)
        work[0:36, :] = from_west[...].astype(F32)[halo : halo + 36]
        work[36:72, :] = from_east[...].astype(F32)[halo : halo + 36]
        target[own : own + 72, :] = work[...].astype(BF)

    @pl.when(first_is_north() == 1)
    def _():
        put(first, LAT - SHIFT, EDGE - 36)
        put(second, 0, 0)

    @pl.when(first_is_north() == 0)
    def _():
        put(first, 0, 0)
        put(second, LAT - SHIFT, EDGE - 36)


def middle(x, gain, w_qkv, w_out, out, x32, stack, normed, q_rows, pairs, queries, context, mixed):
    x32[...] = x[SHIFT : LAT - SHIFT].astype(F32)
    for lat in range(24):
        stack[12 * lat : 12 * lat + 12, :] = x32[lat, 6:18, :]
    attend(stack, gain, w_qkv, w_out, KEYS, normed, q_rows, pairs, queries, context, mixed)
    for lat in range(24):
        x32[lat, 6:18, :] = mixed[12 * lat : 12 * lat + 12, :]
    out[...] = x32[...].astype(BF)


def side_windows(east, x, halo, done, gain, w_qkv, w_out, out, x32, halo32, stack, normed, q_rows, pairs, queries, context, mixed):
    lon = LON - SHIFT if east else 0
    x32[...] = x[SHIFT : LAT - SHIFT].astype(F32)
    halo32[...] = halo[...].astype(F32)
    for band in range(2):
        base = KEYS * band
        for step in range(12):
            stack[base + 6 * step : base + 6 * step + 6, :] = x32[12 * band + step, lon : lon + 6, :]
        stack[base + 72 : base + 144, :] = halo32[36 + 72 * band : 108 + 72 * band, :]
    attend(stack, gain, w_qkv, w_out, HALF, normed, q_rows, pairs, queries, context, mixed)
    x32[...] = done[...].astype(F32)
    for band in range(2):
        for step in range(12):
            x32[12 * band + step, lon : lon + 6, :] = mixed[HALF * band + 6 * step : HALF * band + 6 * step + 6, :]
    out[...] = x32[...].astype(BF)


def west_side(*refs):
    side_windows(False, *refs)


def east_side(*refs):
    side_windows(True, *refs)


def prepare(x, from_west, from_east, gain, w_qkv, raw, queries, pairs, x32, w32, e32, stack, normed):
    x32[0:SHIFT] = x[0:SHIFT].astype(F32)
    x32[SHIFT : 2 * SHIFT] = x[LAT - SHIFT : LAT].astype(F32)
    w32[...] = from_west[...].astype(F32)
    e32[...] = from_east[...].astype(F32)
    for north in range(2):
        base = 3 * HALF * north
        for step in range(SHIFT):
            at = SHIFT * north + step
            stack[base + 12 * step : base + 12 * step + 12, :] = x32[at, 6:18, :]
            stack[base + 80 + 6 * step : base + 86 + 6 * step, :] = x32[at, 0:6, :]
            stack[base + 160 + 6 * step : base + 166 + 6 * step, :] = x32[at, 18:24, :]
        halo = EDGE - 36 if north else 0
        stack[base + 116 : base + 152, :] = w32[halo : halo + 36, :]
        stack[base + 196 : base + 232, :] = e32[halo : halo + 36, :]
        for window in range(3):
            stack[base + 80 * window + 72 : base + 80 * window + 80, :] = jnp.zeros((8, WIDTH), F32)
    raw[...] = stack[...].astype(BF)
    normalise(raw, gain[...], normed, HALF)
    project_pairs(normed, w_qkv, pairs)
    project_queries(normed, w_qkv, queries)


def pole_bias(mask, band, north):
    key = lax.broadcasted_iota(jnp.int32, (1, 2 * HALF), 1)
    in_halo = key >= HALF
    inner = jnp.where(in_halo, key - HALF, key)
    row_wide = inner // 12
    row_corner = jnp.where(inner >= 36, inner - 36, inner) // 6
    real = inner < 72
    bias_wide = jnp.full((1, 2 * HALF), -1e30, F32)
    bias_corner = bias_wide
    lat_at = band * LAT + (LAT - SHIFT) * north
    halo_at = band * LAT + (LAT + SHIFT) * north - SHIFT
    for step in range(SHIFT):
        there = halo_at + step
        exists = jnp.logical_and(there >= 0, there < NLAT)
        halo_ok = jnp.logical_and(exists, mask[jnp.clip(there, 0, NLAT - 1)] == 1)
        own_bias = jnp.where(mask[lat_at + step] == 1, 0.0, -1e30)
        halo_bias = jnp.where(halo_ok, 0.0, -1e30)
        step_bias = jnp.where(in_halo, halo_bias, own_bias)
        bias_wide = jnp.where(jnp.logical_and(real, row_wide == step), step_bias, bias_wide)
        bias_corner = jnp.where(jnp.logical_and(real, row_corner == step), step_bias, bias_corner)
    return bias_wide, bias_corner


def pole_windows(
    north, mask, raw, queries, own_pairs, arrived, gain, w_qkv, w_out, result,
    halo, stack, normed, pairs, context, mixed, x32, copies=(),
):
    halo[...] = arrived[...].astype(F32)
    for step in range(SHIFT):
        at = LON * step
        stack[12 * step : 12 * step + 12, :] = halo[at + 6 : at + 18, :]
        stack[80 + 6 * step : 86 + 6 * step, :] = halo[at : at + 6, :]
        stack[160 + 6 * step : 166 + 6 * step, :] = halo[at + 18 : at + 24, :]
    stack[116:152, :] = halo[144:180, :]
    stack[196:232, :] = halo[180:216, :]
    for window in range(3):
        stack[80 * window + 72 : 80 * window + 80, :] = jnp.zeros((8, WIDTH), F32)
    wide, corner = pole_bias(mask, lax.axis_index("lat"), north)
    normalise(stack, gain[...], normed, HALF)
    project_pairs(normed, w_qkv, pairs)
    base = pl.multiple_of(3 * HALF * north, 3 * HALF)
    for index, bias in enumerate((wide, corner, corner)):
        at = HALF * index
        parts = [(own_pairs, base + at, HALF), (pairs, at, HALF)]
        window_context(queries, base + at, at, HALF, parts, context, bias)
    for col in range(0, WIDTH, 256):
        cols = slice(col, col + 256)
        part = jnp.dot(context[...], w_out[:, cols], preferred_element_type=F32)
        mixed[:, cols] = part + raw[pl.ds(base, 3 * HALF), cols].astype(F32)
        for step in range(SHIFT):
            x32[step, 6:18, cols] = mixed[12 * step : 12 * step + 12, cols]
            x32[step, 0:6, cols] = mixed[80 + 6 * step : 86 + 6 * step, cols]
            x32[step, 18:24, cols] = mixed[160 + 6 * step : 166 + 6 * step, cols]
        result[:, :, cols] = x32[:, :, cols].astype(BF)
        if copies:
            copies[col // 256].start()


def first_pole(*refs):
    pole_windows(first_is_north(), *refs)


def second_pole(mask, raw, queries, own_pairs, arrived, inner, early, gain, w_qkv, w_out, out, *scratch):
    *work, rows, sem = scratch
    north = 1 - first_is_north()
    far = LAT - SHIFT
    copies = [
        pltpu.make_async_copy(inner, out.at[SHIFT : LAT - SHIFT], sem.at[0]),
        pltpu.make_async_copy(early, out.at[pl.ds(far - far * north, SHIFT)], sem.at[1]),
        *(
            pltpu.make_async_copy(
                rows.at[:, :, pl.ds(col, 256)], out.at[pl.ds(far * north, SHIFT), :, pl.ds(col, 256)], sem.at[2 + col // 256]
            )
            for col in range(0, WIDTH, 256)
        ),
    ]
    copies[0].start()
    copies[1].start()
    pole_windows(north, mask, raw, queries, own_pairs, arrived, gain, w_qkv, w_out, rows, *work, copies=copies[2:])
    for copy in copies:
        copy.wait()


def vmem(rows, columns=WIDTH, dtype=BF):
    return pltpu.VMEM((rows, columns), dtype)


def work_space(windows, count):
    total, asked = KEYS * windows, count * windows
    return [
        vmem(total, dtype=F32), vmem(total), vmem(asked), vmem(total, 2 * WIDTH),
        vmem(asked), vmem(asked), vmem(asked, dtype=F32),
    ]


def call(body, out_shape, scratch, flops, *operands, smem=0, in_hbm=False):
    whole = pl.BlockSpec(memory_space=pltpu.VMEM)
    out_spec = pl.BlockSpec(memory_space=pl.ANY) if in_hbm else whole
    specs = [pl.BlockSpec(memory_space=pltpu.SMEM)] * smem + [whole] * (len(operands) - smem)
    return pl.pallas_call(
        body,
        out_shape=out_shape,
        in_specs=specs,
        out_specs=jax.tree.map(lambda _: out_spec, out_shape),
        scratch_shapes=scratch,
        compiler_params=pltpu.CompilerParams(vmem_limit_bytes=40 * 2**20),
        cost_estimate=pl.CostEstimate(flops=flops, bytes_accessed=flops // 1000, transcendentals=0),
    )(*operands)


def shards(tokens, norm_gain, w_qkv, w_out, pole_mask):
    x = jnp.transpose(tokens, (1, 0, 2))
    gain = norm_gain.reshape(1, WIDTH)
    lons, lats = lax.axis_size("lon"), lax.axis_size("lat")
    eastward = [(i, (i + 1) % lons) for i in range(lons)]
    northward = [(i, i + 1) for i in range(lats - 1)]
    edge = jax.ShapeDtypeStruct((EDGE, WIDTH), BF)
    inner = jax.ShapeDtypeStruct((LAT - 2 * SHIFT, LON, WIDTH), BF)
    edge32 = vmem(EDGE, dtype=F32)
    inner32 = pltpu.VMEM((LAT - 2 * SHIFT, LON, WIDTH), F32)
    poles32 = pltpu.VMEM((2 * SHIFT, LON, WIDTH), F32)
    east, west = call(pack_lon, (edge, edge), [edge32, edge32], 8_000_000_000, x)
    from_west = lax.ppermute(east, "lon", eastward)
    from_east = lax.ppermute(west, "lon", [(b, a) for a, b in eastward])
    part = call(middle, inner, [inner32] + work_space(2, KEYS), 2_000_000_000, x, gain, w_qkv, w_out)
    part, from_west = lax.optimization_barrier((part, from_west))
    side_work = [inner32, edge32] + work_space(2, HALF)
    part = call(west_side, inner, side_work, 1_000_000, x, from_west, part, gain, w_qkv, w_out)
    part, from_west, from_east = lax.optimization_barrier((part, from_west, from_east))
    first, second = call(pack_lat, (edge, edge), [vmem(72, dtype=F32)], 1_000_000, x, from_west, from_east)
    met_first = lax.ppermute(first, "lat", [pair for a, b in northward[0::2] for pair in ((a, b), (b, a))])
    met_second = lax.ppermute(second, "lat", [pair for a, b in northward[1::2] for pair in ((a, b), (b, a))])
    part = call(east_side, inner, side_work, 1_000_000, x, from_east, part, gain, w_qkv, w_out)
    rows = 6 * HALF
    raw, queries, pairs = call(
        prepare, tuple(jax.ShapeDtypeStruct((rows, n), BF) for n in (WIDTH, WIDTH, 2 * WIDTH)),
        [poles32, edge32, edge32, vmem(rows, dtype=F32), vmem(rows)], 1_000_000,
        x, from_west, from_east, gain, w_qkv,
    )
    half = rows // 2
    work = [edge32, vmem(half, dtype=F32), vmem(half), vmem(half, 2 * WIDTH), vmem(half), vmem(half, dtype=F32)]
    work.append(pltpu.VMEM((SHIFT, LON, WIDTH), F32))
    part, met_first = lax.optimization_barrier((part, met_first))
    early = call(
        first_pole, jax.ShapeDtypeStruct((SHIFT, LON, WIDTH), BF), work, 1_000_000,
        pole_mask, raw, queries, pairs, met_first, gain, w_qkv, w_out, smem=1,
    )
    early, met_second = lax.optimization_barrier((early, met_second))
    mixed = call(
        second_pole, jax.ShapeDtypeStruct((LAT, LON, WIDTH), BF),
        work + [pltpu.VMEM((SHIFT, LON, WIDTH), BF), pltpu.SemaphoreType.DMA((4,))], 2_000_000_000,
        pole_mask, raw, queries, pairs, met_second, part, early, gain, w_qkv, w_out, smem=1, in_hbm=True,
    )
    return jnp.transpose(mixed, (1, 0, 2))


def solution(mesh):
    in_specs = (P("lon", "lat", None), P(), P(), P(), P())
    out_specs = P("lon", "lat", None)
    return jax.shard_map(shards, mesh=mesh, in_specs=in_specs, out_specs=out_specs, check_vma=False)
```

```python
import functools

import jax
import jax.numpy as jnp
from jax import lax
from jax.experimental import pallas as pl
from jax.experimental.pallas import tpu as pltpu
from jax.sharding import PartitionSpec as P

WIDTH = 512
HEADS = 8
WINDOW = 12
SHIFT = 6
KEYS = WINDOW * WINDOW
EPS = 1e-05
NLAT = 288
LON = 24
LAT = 36
EDGE = LAT * SHIFT
HALF = 80
BF = jnp.bfloat16
F32 = jnp.float32


def normalise(window_tokens, gain, normed, block):
    for start in range(0, normed.shape[0], block):
        values = window_tokens[start : start + block, :].astype(F32)
        average = jnp.sum(values, axis=-1, keepdims=True) * (1.0 / WIDTH)
        centred = values - average
        variance = jnp.sum(centred * centred, axis=-1, keepdims=True) * (1.0 / WIDTH)
        normed[start : start + block, :] = (centred * lax.rsqrt(variance + EPS) * gain).astype(BF)


def project_pairs(normed, w_qkv, pairs):
    for col in range(0, 2 * WIDTH, 256):
        part = jnp.dot(normed[...], w_qkv[:, WIDTH + col : WIDTH + col + 256], preferred_element_type=F32)
        pairs[:, col : col + 256] = part.astype(BF)


def project_queries(rows, w_qkv, queries):
    for col in range(0, WIDTH, 256):
        part = jnp.dot(rows[...], w_qkv[:, col : col + 256], preferred_element_type=F32)
        queries[:, col : col + 256] = (part.astype(BF).astype(F32) * (WIDTH // HEADS) ** (-0.5)).astype(BF)


def window_context(queries, q_base, c_base, count, key_parts, context, bias):
    lane = lax.broadcasted_iota(jnp.int32, (1, 128), 1)
    low32 = lane < 64
    keep_low = low32.astype(F32).astype(BF)
    keep_high = (lane >= 64).astype(F32).astype(BF)
    ones = jnp.ones((sum(part[2] for part in key_parts), 128), BF)

    def rows_of(col):
        found = [ref[pl.ds(base, rows), col : col + 128] for ref, base, rows in key_parts]
        return found[0] if len(found) == 1 else jnp.concatenate(found, axis=0)

    for pair in range(HEADS // 2):
        cols = slice(128 * pair, 128 * pair + 128)
        both = queries[pl.ds(q_base, count), cols]
        stacked = jnp.concatenate([both * keep_low, both * keep_high], axis=0)
        key_part, value_part = rows_of(128 * pair), rows_of(WIDTH + 128 * pair)
        scores = lax.dot_general(stacked, key_part, (((1,), (1,)), ((), ())), preferred_element_type=F32)
        if bias is not None:
            scores = scores + bias
        row_max = jnp.max(scores, axis=-1, keepdims=True)
        exp_scores = jnp.exp(scores - row_max).astype(BF)
        widened = jnp.concatenate([value_part, ones], axis=1)
        summed = jnp.dot(exp_scores, widened, preferred_element_type=F32)
        first, second = summed[:count], summed[count:]
        top = jnp.where(low32, first[:, :128], second[:, :128])
        under = jnp.where(low32, first[:, 128:], second[:, 128:])
        context[c_base : c_base + count, cols] = (top / under).astype(BF)


def finish(context, w_out, residual, base, stride, count, mixed):
    for col in range(0, WIDTH, 256):
        part = jnp.dot(context[...], w_out[:, col : col + 256], preferred_element_type=F32)
        for index in range(mixed.shape[0] // count):
            here = slice(count * index, count * index + count)
            own = residual[pl.ds(base + stride * index, count), col : col + 256].astype(F32)
            mixed[here, col : col + 256] = part[here] + own


def attend(window_tokens, gain_ref, w_qkv, w_out, count, normed, q_rows, pairs, queries, context, mixed):
    windows = normed.shape[0] // KEYS
    normalise(window_tokens, gain_ref[...], normed, KEYS)
    for index in range(windows):
        q_rows[count * index : count * index + count, :] = normed[KEYS * index : KEYS * index + count, :]
    project_pairs(normed, w_qkv, pairs)
    project_queries(q_rows, w_qkv, queries)
    for index in range(windows):
        window_context(queries, count * index, count * index, count, [(pairs, KEYS * index, KEYS)], context, None)
    finish(context, w_out, window_tokens, 0, KEYS, count, mixed)


def pack_lon(x, east, west, east32, west32):
    for lat in range(LAT):
        row = x[lat].astype(F32)
        west32[SHIFT * lat : SHIFT * lat + SHIFT, :] = row[0:SHIFT]
        east32[SHIFT * lat : SHIFT * lat + SHIFT, :] = row[LON - SHIFT : LON]
    west[...] = west32[...].astype(BF)
    east[...] = east32[...].astype(BF)


def first_is_north():
    return 1 - lax.axis_index("lat") % 2


def pack_lat(x, from_west, from_east, first, second, work):
    own = SHIFT * LON

    def put(target, lat, halo):
        target[0:own, :] = x[lat : lat + SHIFT].reshape(own, WIDTH)
        work[0:36, :] = from_west[...].astype(F32)[halo : halo + 36]
        work[36:72, :] = from_east[...].astype(F32)[halo : halo + 36]
        target[own : own + 72, :] = work[...].astype(BF)

    @pl.when(first_is_north() == 1)
    def _():
        put(first, LAT - SHIFT, EDGE - 36)
        put(second, 0, 0)

    @pl.when(first_is_north() == 0)
    def _():
        put(first, 0, 0)
        put(second, LAT - SHIFT, EDGE - 36)


def middle(x, gain, w_qkv, w_out, out, x32, stack, normed, q_rows, pairs, queries, context, mixed):
    for lat in range(24):
        stack[12 * lat : 12 * lat + 12, :] = x[SHIFT + lat].astype(F32)[6:18]
    attend(stack, gain, w_qkv, w_out, KEYS, normed, q_rows, pairs, queries, context, mixed)
    for lat in range(24):
        x32[lat, 6:18, :] = mixed[12 * lat : 12 * lat + 12, :]
    out[...] = x32[...].astype(BF)


def side_windows(east, x, halo, done, gain, w_qkv, w_out, out, x32, halo32, stack, normed, q_rows, pairs, queries, context, mixed):
    lon = LON - SHIFT if east else 0
    halo32[...] = halo[...].astype(F32)
    for band in range(2):
        base = KEYS * band
        for step in range(12):
            stack[base + 6 * step : base + 6 * step + 6, :] = x[SHIFT + 12 * band + step].astype(F32)[lon : lon + 6]
        stack[base + 72 : base + 144, :] = halo32[36 + 72 * band : 108 + 72 * band, :]
    attend(stack, gain, w_qkv, w_out, HALF, normed, q_rows, pairs, queries, context, mixed)
    x32[...] = done[...].astype(F32)
    for band in range(2):
        for step in range(12):
            x32[12 * band + step, lon : lon + 6, :] = mixed[HALF * band + 6 * step : HALF * band + 6 * step + 6, :]
    out[...] = x32[...].astype(BF)


def west_side(*refs):
    side_windows(False, *refs)


def east_side(*refs):
    side_windows(True, *refs)


def prepare(x, from_west, from_east, gain, w_qkv, raw, queries, pairs, x32, w32, e32, stack, normed):
    x32[0:SHIFT] = x[0:SHIFT].astype(F32)
    x32[SHIFT : 2 * SHIFT] = x[LAT - SHIFT : LAT].astype(F32)
    w32[...] = from_west[...].astype(F32)
    e32[...] = from_east[...].astype(F32)
    for north in range(2):
        base = 3 * HALF * north
        for step in range(SHIFT):
            at = SHIFT * north + step
            stack[base + 12 * step : base + 12 * step + 12, :] = x32[at, 6:18, :]
            stack[base + 80 + 6 * step : base + 86 + 6 * step, :] = x32[at, 0:6, :]
            stack[base + 160 + 6 * step : base + 166 + 6 * step, :] = x32[at, 18:24, :]
        halo = EDGE - 36 if north else 0
        stack[base + 116 : base + 152, :] = w32[halo : halo + 36, :]
        stack[base + 196 : base + 232, :] = e32[halo : halo + 36, :]
        for window in range(3):
            stack[base + 80 * window + 72 : base + 80 * window + 80, :] = jnp.zeros((8, WIDTH), F32)
    raw[...] = stack[...].astype(BF)
    normalise(raw, gain[...], normed, HALF)
    project_pairs(normed, w_qkv, pairs)
    project_queries(normed, w_qkv, queries)


def pole_bias(mask, band, north):
    key = lax.broadcasted_iota(jnp.int32, (1, 2 * HALF), 1)
    in_halo = key >= HALF
    inner = jnp.where(in_halo, key - HALF, key)
    row_wide = inner // 12
    row_corner = jnp.where(inner >= 36, inner - 36, inner) // 6
    real = inner < 72
    bias_wide = jnp.full((1, 2 * HALF), -1e30, F32)
    bias_corner = bias_wide
    lat_at = band * LAT + (LAT - SHIFT) * north
    halo_at = band * LAT + (LAT + SHIFT) * north - SHIFT
    for step in range(SHIFT):
        there = halo_at + step
        exists = jnp.logical_and(there >= 0, there < NLAT)
        halo_ok = jnp.logical_and(exists, mask[jnp.clip(there, 0, NLAT - 1)] == 1)
        own_bias = jnp.where(mask[lat_at + step] == 1, 0.0, -1e30)
        halo_bias = jnp.where(halo_ok, 0.0, -1e30)
        step_bias = jnp.where(in_halo, halo_bias, own_bias)
        bias_wide = jnp.where(jnp.logical_and(real, row_wide == step), step_bias, bias_wide)
        bias_corner = jnp.where(jnp.logical_and(real, row_corner == step), step_bias, bias_corner)
    return bias_wide, bias_corner


def pole_windows(
    north, mask, raw, queries, own_pairs, arrived, gain, w_qkv, w_out, result,
    halo, stack, normed, pairs, context, mixed, x32,
):
    halo[...] = arrived[...].astype(F32)
    for step in range(SHIFT):
        at = LON * step
        stack[12 * step : 12 * step + 12, :] = halo[at + 6 : at + 18, :]
        stack[80 + 6 * step : 86 + 6 * step, :] = halo[at : at + 6, :]
        stack[160 + 6 * step : 166 + 6 * step, :] = halo[at + 18 : at + 24, :]
    stack[116:152, :] = halo[144:180, :]
    stack[196:232, :] = halo[180:216, :]
    for window in range(3):
        stack[80 * window + 72 : 80 * window + 80, :] = jnp.zeros((8, WIDTH), F32)
    wide, corner = pole_bias(mask, lax.axis_index("lat"), north)
    normalise(stack, gain[...], normed, HALF)
    project_pairs(normed, w_qkv, pairs)
    base = pl.multiple_of(3 * HALF * north, 3 * HALF)
    for index, bias in enumerate((wide, corner, corner)):
        at = HALF * index
        parts = [(own_pairs, base + at, HALF), (pairs, at, HALF)]
        window_context(queries, base + at, at, HALF, parts, context, bias)
    finish(context, w_out, raw, base, HALF, HALF, mixed)
    for step in range(SHIFT):
        x32[step, 6:18, :] = mixed[12 * step : 12 * step + 12, :]
        x32[step, 0:6, :] = mixed[80 + 6 * step : 86 + 6 * step, :]
        x32[step, 18:24, :] = mixed[160 + 6 * step : 166 + 6 * step, :]
    result[...] = x32[...].astype(BF)


def first_pole(*refs):
    pole_windows(first_is_north(), *refs)


def second_pole(mask, raw, queries, own_pairs, arrived, inner, early, gain, w_qkv, w_out, out, *scratch):
    *work, rows, sem = scratch
    north = 1 - first_is_north()
    far = LAT - SHIFT
    copies = [
        pltpu.make_async_copy(inner, out.at[SHIFT : LAT - SHIFT], sem.at[0]),
        pltpu.make_async_copy(early, out.at[pl.ds(far - far * north, SHIFT)], sem.at[1]),
        pltpu.make_async_copy(rows, out.at[pl.ds(far * north, SHIFT)], sem.at[2]),
    ]
    copies[0].start()
    copies[1].start()
    pole_windows(north, mask, raw, queries, own_pairs, arrived, gain, w_qkv, w_out, rows, *work)
    copies[2].start()
    for copy in copies:
        copy.wait()


def vmem(rows, columns=WIDTH, dtype=BF):
    return pltpu.VMEM((rows, columns), dtype)


def work_space(windows, count):
    total, asked = KEYS * windows, count * windows
    return [
        vmem(total, dtype=F32), vmem(total), vmem(asked), vmem(total, 2 * WIDTH),
        vmem(asked), vmem(asked), vmem(asked, dtype=F32),
    ]


def call(body, out_shape, scratch, flops, *operands, smem=0, in_hbm=False):
    whole = pl.BlockSpec(memory_space=pltpu.VMEM)
    out_spec = pl.BlockSpec(memory_space=pl.ANY) if in_hbm else whole
    specs = [pl.BlockSpec(memory_space=pltpu.SMEM)] * smem + [whole] * (len(operands) - smem)
    return pl.pallas_call(
        body,
        out_shape=out_shape,
        in_specs=specs,
        out_specs=jax.tree.map(lambda _: out_spec, out_shape),
        scratch_shapes=scratch,
        compiler_params=pltpu.CompilerParams(vmem_limit_bytes=40 * 2**20),
        cost_estimate=pl.CostEstimate(flops=flops, bytes_accessed=flops // 1000, transcendentals=0),
    )(*operands)


def shards(tokens, norm_gain, w_qkv, w_out, pole_mask):
    x = jnp.transpose(tokens, (1, 0, 2))
    gain = norm_gain.reshape(1, WIDTH)
    lons, lats = lax.axis_size("lon"), lax.axis_size("lat")
    eastward = [(i, (i + 1) % lons) for i in range(lons)]
    northward = [(i, i + 1) for i in range(lats - 1)]
    edge = jax.ShapeDtypeStruct((EDGE, WIDTH), BF)
    inner = jax.ShapeDtypeStruct((LAT - 2 * SHIFT, LON, WIDTH), BF)
    edge32 = vmem(EDGE, dtype=F32)
    inner32 = pltpu.VMEM((LAT - 2 * SHIFT, LON, WIDTH), F32)
    poles32 = pltpu.VMEM((2 * SHIFT, LON, WIDTH), F32)
    east, west = call(pack_lon, (edge, edge), [edge32, edge32], 8_000_000_000, x)
    from_west = lax.ppermute(east, "lon", eastward)
    from_east = lax.ppermute(west, "lon", [(b, a) for a, b in eastward])
    part = call(middle, inner, [inner32] + work_space(2, KEYS), 2_000_000_000, x, gain, w_qkv, w_out)
    part, from_west = lax.optimization_barrier((part, from_west))
    side_work = [inner32, edge32] + work_space(2, HALF)
    part = call(west_side, inner, side_work, 1_000_000, x, from_west, part, gain, w_qkv, w_out)
    part, from_west, from_east = lax.optimization_barrier((part, from_west, from_east))
    first, second = call(pack_lat, (edge, edge), [vmem(72, dtype=F32)], 1_000_000, x, from_west, from_east)
    met_first = lax.ppermute(first, "lat", [pair for a, b in northward[0::2] for pair in ((a, b), (b, a))])
    met_second = lax.ppermute(second, "lat", [pair for a, b in northward[1::2] for pair in ((a, b), (b, a))])
    part = call(east_side, inner, side_work, 1_000_000, x, from_east, part, gain, w_qkv, w_out)
    rows = 6 * HALF
    raw, queries, pairs = call(
        prepare, tuple(jax.ShapeDtypeStruct((rows, n), BF) for n in (WIDTH, WIDTH, 2 * WIDTH)),
        [poles32, edge32, edge32, vmem(rows, dtype=F32), vmem(rows)], 1_000_000,
        x, from_west, from_east, gain, w_qkv,
    )
    half = rows // 2
    work = [edge32, vmem(half, dtype=F32), vmem(half), vmem(half, 2 * WIDTH), vmem(half), vmem(half, dtype=F32)]
    work.append(pltpu.VMEM((SHIFT, LON, WIDTH), F32))
    part, met_first = lax.optimization_barrier((part, met_first))
    early = call(
        first_pole, jax.ShapeDtypeStruct((SHIFT, LON, WIDTH), BF), work, 1_000_000,
        pole_mask, raw, queries, pairs, met_first, gain, w_qkv, w_out, smem=1,
    )
    early, met_second = lax.optimization_barrier((early, met_second))
    mixed = call(
        second_pole, jax.ShapeDtypeStruct((LAT, LON, WIDTH), BF),
        work + [pltpu.VMEM((SHIFT, LON, WIDTH), BF), pltpu.SemaphoreType.DMA((3,))], 2_000_000_000,
        pole_mask, raw, queries, pairs, met_second, part, early, gain, w_qkv, w_out, smem=1, in_hbm=True,
    )
    return jnp.transpose(mixed, (1, 0, 2))


def solution(mesh):
    in_specs = (P("lon", "lat", None), P(), P(), P(), P())
    out_specs = P("lon", "lat", None)
    return jax.shard_map(shards, mesh=mesh, in_specs=in_specs, out_specs=out_specs, check_vma=False)
```

```python
import functools

import jax
import jax.numpy as jnp
from jax import lax
from jax.experimental import pallas as pl
from jax.experimental.pallas import tpu as pltpu
from jax.sharding import PartitionSpec as P

WIDTH = 512
HEADS = 8
WINDOW = 12
SHIFT = 6
KEYS = WINDOW * WINDOW
EPS = 1e-05
NLAT = 288
LON = 24
LAT = 36
EDGE = LAT * SHIFT
HALF = 80
BF = jnp.bfloat16
F32 = jnp.float32


def normalise(window_tokens, gain, normed, block):
    for start in range(0, normed.shape[0], block):
        values = window_tokens[start : start + block, :].astype(F32)
        average = jnp.sum(values, axis=-1, keepdims=True) * (1.0 / WIDTH)
        centred = values - average
        variance = jnp.sum(centred * centred, axis=-1, keepdims=True) * (1.0 / WIDTH)
        normed[start : start + block, :] = (centred * lax.rsqrt(variance + EPS) * gain).astype(BF)


def project_pairs(normed, w_qkv, pairs):
    for col in range(0, 2 * WIDTH, 256):
        part = jnp.dot(normed[...], w_qkv[:, WIDTH + col : WIDTH + col + 256], preferred_element_type=F32)
        pairs[:, col : col + 256] = part.astype(BF)


def project_queries(rows, w_qkv, queries):
    for col in range(0, WIDTH, 256):
        part = jnp.dot(rows[...], w_qkv[:, col : col + 256], preferred_element_type=F32)
        queries[:, col : col + 256] = (part.astype(BF).astype(F32) * (WIDTH // HEADS) ** (-0.5)).astype(BF)


def window_context(queries, q_base, c_base, count, key_parts, context, bias):
    lane = lax.broadcasted_iota(jnp.int32, (1, 128), 1)
    low32 = lane < 64
    keep_low = low32.astype(F32).astype(BF)
    keep_high = (lane >= 64).astype(F32).astype(BF)
    ones = jnp.ones((sum(part[2] for part in key_parts), 128), BF)

    def rows_of(col):
        found = [ref[pl.ds(base, rows), col : col + 128] for ref, base, rows in key_parts]
        return found[0] if len(found) == 1 else jnp.concatenate(found, axis=0)

    for pair in range(HEADS // 2):
        cols = slice(128 * pair, 128 * pair + 128)
        both = queries[pl.ds(q_base, count), cols]
        stacked = jnp.concatenate([both * keep_low, both * keep_high], axis=0)
        key_part, value_part = rows_of(128 * pair), rows_of(WIDTH + 128 * pair)
        scores = lax.dot_general(stacked, key_part, (((1,), (1,)), ((), ())), preferred_element_type=F32)
        if bias is not None:
            scores = scores + bias
        row_max = jnp.max(scores, axis=-1, keepdims=True)
        exp_scores = jnp.exp(scores - row_max).astype(BF)
        widened = jnp.concatenate([value_part, ones], axis=1)
        summed = jnp.dot(exp_scores, widened, preferred_element_type=F32)
        first, second = summed[:count], summed[count:]
        top = jnp.where(low32, first[:, :128], second[:, :128])
        under = jnp.where(low32, first[:, 128:], second[:, 128:])
        context[c_base : c_base + count, cols] = (top / under).astype(BF)


def finish(context, w_out, residual, base, stride, count, mixed):
    for col in range(0, WIDTH, 256):
        part = jnp.dot(context[...], w_out[:, col : col + 256], preferred_element_type=F32)
        for index in range(mixed.shape[0] // count):
            here = slice(count * index, count * index + count)
            own = residual[pl.ds(base + stride * index, count), col : col + 256].astype(F32)
            mixed[here, col : col + 256] = part[here] + own


def attend(window_tokens, gain_ref, w_qkv, w_out, count, normed, q_rows, pairs, queries, context, mixed):
    windows = normed.shape[0] // KEYS
    normalise(window_tokens, gain_ref[...], normed, KEYS)
    for index in range(windows):
        q_rows[count * index : count * index + count, :] = normed[KEYS * index : KEYS * index + count, :]
    project_pairs(normed, w_qkv, pairs)
    project_queries(q_rows, w_qkv, queries)
    for index in range(windows):
        window_context(queries, count * index, count * index, count, [(pairs, KEYS * index, KEYS)], context, None)
    finish(context, w_out, window_tokens, 0, KEYS, count, mixed)


def pack_lon(x, east, west, east32, west32):
    for lat in range(LAT):
        row = x[lat].astype(F32)
        west32[SHIFT * lat : SHIFT * lat + SHIFT, :] = row[0:SHIFT]
        east32[SHIFT * lat : SHIFT * lat + SHIFT, :] = row[LON - SHIFT : LON]
    west[...] = west32[...].astype(BF)
    east[...] = east32[...].astype(BF)


def first_is_north():
    return 1 - lax.axis_index("lat") % 2


def pack_lat(x, from_west, from_east, first, second, work):
    own = SHIFT * LON

    def put(target, lat, halo):
        target[0:own, :] = x[lat : lat + SHIFT].reshape(own, WIDTH)
        work[0:36, :] = from_west[...].astype(F32)[halo : halo + 36]
        work[36:72, :] = from_east[...].astype(F32)[halo : halo + 36]
        target[own : own + 72, :] = work[...].astype(BF)

    @pl.when(first_is_north() == 1)
    def _():
        put(first, LAT - SHIFT, EDGE - 36)
        put(second, 0, 0)

    @pl.when(first_is_north() == 0)
    def _():
        put(first, 0, 0)
        put(second, LAT - SHIFT, EDGE - 36)


def middle(x, gain, w_qkv, w_out, out, x32, stack, normed, q_rows, pairs, queries, context, mixed):
    for lat in range(24):
        stack[12 * lat : 12 * lat + 12, :] = x[SHIFT + lat].astype(F32)[6:18]
    attend(stack, gain, w_qkv, w_out, KEYS, normed, q_rows, pairs, queries, context, mixed)
    for lat in range(24):
        x32[lat, 6:18, :] = mixed[12 * lat : 12 * lat + 12, :]
    out[...] = x32[...].astype(BF)


def side_windows(east, x, halo, done, gain, w_qkv, w_out, out, x32, halo32, stack, normed, q_rows, pairs, queries, context, mixed):
    lon = LON - SHIFT if east else 0
    halo32[...] = halo[...].astype(F32)
    for band in range(2):
        base = KEYS * band
        for step in range(12):
            stack[base + 6 * step : base + 6 * step + 6, :] = x[SHIFT + 12 * band + step].astype(F32)[lon : lon + 6]
        stack[base + 72 : base + 144, :] = halo32[36 + 72 * band : 108 + 72 * band, :]
    attend(stack, gain, w_qkv, w_out, HALF, normed, q_rows, pairs, queries, context, mixed)
    x32[...] = done[...].astype(F32)
    for band in range(2):
        for step in range(12):
            x32[12 * band + step, lon : lon + 6, :] = mixed[HALF * band + 6 * step : HALF * band + 6 * step + 6, :]
    out[...] = x32[...].astype(BF)


def west_side(*refs):
    side_windows(False, *refs)


def east_side(*refs):
    side_windows(True, *refs)


def prepare(x, from_west, from_east, gain, w_qkv, raw, queries, pairs, x32, w32, e32, stack, normed):
    x32[0:SHIFT] = x[0:SHIFT].astype(F32)
    x32[SHIFT : 2 * SHIFT] = x[LAT - SHIFT : LAT].astype(F32)
    w32[...] = from_west[...].astype(F32)
    e32[...] = from_east[...].astype(F32)
    for north in range(2):
        base = 3 * HALF * north
        for step in range(SHIFT):
            at = SHIFT * north + step
            stack[base + 12 * step : base + 12 * step + 12, :] = x32[at, 6:18, :]
            stack[base + 80 + 6 * step : base + 86 + 6 * step, :] = x32[at, 0:6, :]
            stack[base + 160 + 6 * step : base + 166 + 6 * step, :] = x32[at, 18:24, :]
        halo = EDGE - 36 if north else 0
        stack[base + 116 : base + 152, :] = w32[halo : halo + 36, :]
        stack[base + 196 : base + 232, :] = e32[halo : halo + 36, :]
        for window in range(3):
            stack[base + 80 * window + 72 : base + 80 * window + 80, :] = jnp.zeros((8, WIDTH), F32)
    raw[...] = stack[...].astype(BF)
    normalise(raw, gain[...], normed, HALF)
    project_pairs(normed, w_qkv, pairs)
    project_queries(normed, w_qkv, queries)


def pole_bias(mask, band, north):
    key = lax.broadcasted_iota(jnp.int32, (1, 2 * HALF), 1)
    in_halo = key >= HALF
    inner = jnp.where(in_halo, key - HALF, key)
    row_wide = inner // 12
    row_corner = jnp.where(inner >= 36, inner - 36, inner) // 6
    real = inner < 72
    bias_wide = jnp.full((1, 2 * HALF), -1e30, F32)
    bias_corner = bias_wide
    lat_at = band * LAT + (LAT - SHIFT) * north
    halo_at = band * LAT + (LAT + SHIFT) * north - SHIFT
    for step in range(SHIFT):
        there = halo_at + step
        exists = jnp.logical_and(there >= 0, there < NLAT)
        halo_ok = jnp.logical_and(exists, mask[jnp.clip(there, 0, NLAT - 1)] == 1)
        own_bias = jnp.where(mask[lat_at + step] == 1, 0.0, -1e30)
        halo_bias = jnp.where(halo_ok, 0.0, -1e30)
        step_bias = jnp.where(in_halo, halo_bias, own_bias)
        bias_wide = jnp.where(jnp.logical_and(real, row_wide == step), step_bias, bias_wide)
        bias_corner = jnp.where(jnp.logical_and(real, row_corner == step), step_bias, bias_corner)
    return bias_wide, bias_corner


def pole_windows(
    north, mask, raw, queries, own_pairs, arrived, gain, w_qkv, w_out, result,
    halo, stack, normed, pairs, context, mixed, x32, copies=(),
):
    halo[...] = arrived[...].astype(F32)
    for step in range(SHIFT):
        at = LON * step
        stack[12 * step : 12 * step + 12, :] = halo[at + 6 : at + 18, :]
        stack[80 + 6 * step : 86 + 6 * step, :] = halo[at : at + 6, :]
        stack[160 + 6 * step : 166 + 6 * step, :] = halo[at + 18 : at + 24, :]
    stack[116:152, :] = halo[144:180, :]
    stack[196:232, :] = halo[180:216, :]
    for window in range(3):
        stack[80 * window + 72 : 80 * window + 80, :] = jnp.zeros((8, WIDTH), F32)
    wide, corner = pole_bias(mask, lax.axis_index("lat"), north)
    normalise(stack, gain[...], normed, HALF)
    project_pairs(normed, w_qkv, pairs)
    base = pl.multiple_of(3 * HALF * north, 3 * HALF)
    for index, bias in enumerate((wide, corner, corner)):
        at = HALF * index
        parts = [(own_pairs, base + at, HALF), (pairs, at, HALF)]
        window_context(queries, base + at, at, HALF, parts, context, bias)
    for col in range(0, WIDTH, 256):
        cols = slice(col, col + 256)
        part = jnp.dot(context[...], w_out[:, cols], preferred_element_type=F32)
        mixed[:, cols] = part + raw[pl.ds(base, 3 * HALF), cols].astype(F32)
        for step in range(SHIFT):
            x32[step, 6:18, cols] = mixed[12 * step : 12 * step + 12, cols]
            x32[step, 0:6, cols] = mixed[80 + 6 * step : 86 + 6 * step, cols]
            x32[step, 18:24, cols] = mixed[160 + 6 * step : 166 + 6 * step, cols]
        result[:, :, cols] = x32[:, :, cols].astype(BF)
        if copies:
            copies[col // 256].start()


def first_pole(*refs):
    pole_windows(first_is_north(), *refs)


def second_pole(mask, raw, queries, own_pairs, arrived, inner, early, gain, w_qkv, w_out, out, *scratch):
    *work, rows, sem = scratch
    north = 1 - first_is_north()
    far = LAT - SHIFT
    copies = [
        pltpu.make_async_copy(inner, out.at[SHIFT : LAT - SHIFT], sem.at[0]),
        pltpu.make_async_copy(early, out.at[pl.ds(far - far * north, SHIFT)], sem.at[1]),
        *(
            pltpu.make_async_copy(
                rows.at[:, :, pl.ds(col, 256)], out.at[pl.ds(far * north, SHIFT), :, pl.ds(col, 256)], sem.at[2 + col // 256]
            )
            for col in range(0, WIDTH, 256)
        ),
    ]
    copies[0].start()
    copies[1].start()
    pole_windows(north, mask, raw, queries, own_pairs, arrived, gain, w_qkv, w_out, rows, *work, copies=copies[2:])
    for copy in copies:
        copy.wait()


def vmem(rows, columns=WIDTH, dtype=BF):
    return pltpu.VMEM((rows, columns), dtype)


def work_space(windows, count):
    total, asked = KEYS * windows, count * windows
    return [
        vmem(total, dtype=F32), vmem(total), vmem(asked), vmem(total, 2 * WIDTH),
        vmem(asked), vmem(asked), vmem(asked, dtype=F32),
    ]


def call(body, out_shape, scratch, flops, *operands, smem=0, in_hbm=False):
    whole = pl.BlockSpec(memory_space=pltpu.VMEM)
    out_spec = pl.BlockSpec(memory_space=pl.ANY) if in_hbm else whole
    specs = [pl.BlockSpec(memory_space=pltpu.SMEM)] * smem + [whole] * (len(operands) - smem)
    return pl.pallas_call(
        body,
        out_shape=out_shape,
        in_specs=specs,
        out_specs=jax.tree.map(lambda _: out_spec, out_shape),
        scratch_shapes=scratch,
        compiler_params=pltpu.CompilerParams(vmem_limit_bytes=40 * 2**20),
        cost_estimate=pl.CostEstimate(flops=flops, bytes_accessed=flops // 1000, transcendentals=0),
    )(*operands)


def shards(tokens, norm_gain, w_qkv, w_out, pole_mask):
    x = jnp.transpose(tokens, (1, 0, 2))
    gain = norm_gain.reshape(1, WIDTH)
    lons, lats = lax.axis_size("lon"), lax.axis_size("lat")
    eastward = [(i, (i + 1) % lons) for i in range(lons)]
    northward = [(i, i + 1) for i in range(lats - 1)]
    edge = jax.ShapeDtypeStruct((EDGE, WIDTH), BF)
    inner = jax.ShapeDtypeStruct((LAT - 2 * SHIFT, LON, WIDTH), BF)
    edge32 = vmem(EDGE, dtype=F32)
    inner32 = pltpu.VMEM((LAT - 2 * SHIFT, LON, WIDTH), F32)
    poles32 = pltpu.VMEM((2 * SHIFT, LON, WIDTH), F32)
    east, west = call(pack_lon, (edge, edge), [edge32, edge32], 8_000_000_000, x)
    from_west = lax.ppermute(east, "lon", eastward)
    from_east = lax.ppermute(west, "lon", [(b, a) for a, b in eastward])
    part = call(middle, inner, [inner32] + work_space(2, KEYS), 2_000_000_000, x, gain, w_qkv, w_out)
    part, from_west = lax.optimization_barrier((part, from_west))
    side_work = [inner32, edge32] + work_space(2, HALF)
    part = call(west_side, inner, side_work, 1_000_000, x, from_west, part, gain, w_qkv, w_out)
    part, from_west, from_east = lax.optimization_barrier((part, from_west, from_east))
    first, second = call(pack_lat, (edge, edge), [vmem(72, dtype=F32)], 1_000_000, x, from_west, from_east)
    met_first = lax.ppermute(first, "lat", [pair for a, b in northward[0::2] for pair in ((a, b), (b, a))])
    met_second = lax.ppermute(second, "lat", [pair for a, b in northward[1::2] for pair in ((a, b), (b, a))])
    part = call(east_side, inner, side_work, 1_000_000, x, from_east, part, gain, w_qkv, w_out)
    rows = 6 * HALF
    raw, queries, pairs = call(
        prepare, tuple(jax.ShapeDtypeStruct((rows, n), BF) for n in (WIDTH, WIDTH, 2 * WIDTH)),
        [poles32, edge32, edge32, vmem(rows, dtype=F32), vmem(rows)], 1_000_000,
        x, from_west, from_east, gain, w_qkv,
    )
    half = rows // 2
    work = [edge32, vmem(half, dtype=F32), vmem(half), vmem(half, 2 * WIDTH), vmem(half), vmem(half, dtype=F32)]
    work.append(pltpu.VMEM((SHIFT, LON, WIDTH), F32))
    part, met_first = lax.optimization_barrier((part, met_first))
    early = call(
        first_pole, jax.ShapeDtypeStruct((SHIFT, LON, WIDTH), BF), work, 1_000_000,
        pole_mask, raw, queries, pairs, met_first, gain, w_qkv, w_out, smem=1,
    )
    early, met_second = lax.optimization_barrier((early, met_second))
    mixed = call(
        second_pole, jax.ShapeDtypeStruct((LAT, LON, WIDTH), BF),
        work + [pltpu.VMEM((SHIFT, LON, WIDTH), BF), pltpu.SemaphoreType.DMA((4,))], 2_000_000_000,
        pole_mask, raw, queries, pairs, met_second, part, early, gain, w_qkv, w_out, smem=1, in_hbm=True,
    )
    return jnp.transpose(mixed, (1, 0, 2))


def solution(mesh):
    in_specs = (P("lon", "lat", None), P(), P(), P(), P())
    out_specs = P("lon", "lat", None)
    return jax.shard_map(shards, mesh=mesh, in_specs=in_specs, out_specs=out_specs, check_vma=False)
```
